32 devices in a mesh: wall: 2 (over x), plane: 16 (over z, y, core).
Axes of the slice: x: 2, y: 2, z: 4, core: 2. Of those that a mesh axis runs over, the one named last changes fastest.
Arguments:
- jacobian: float32 [3, 16, 16, 32, 16, 128], P(None, None, None, 'wall', 'plane'), as said below
- residual: float32 [16, 32, 16, 128], P(None, 'wall', 'plane')
- previous_update: float32 [16, 32, 16, 128], P(None, 'wall', 'plane'), may hold values from -6 to 6
- offline_coupling: float32 [4, 16, 32, 16, 128], P(None, None, 'wall', 'plane'), may hold values from 0.003 to 0.03
- wake_partner: int32 [16, 128], P('plane'), may hold values from 0 to 127, each once within a row
- line_length: int32 [16, 128], P('plane'), may hold values from 16 to 32
- bottom_flag: int32 [16, 128], P('plane'), may hold values 0 or 1
Outputs:
- update: float32 [16, 32, 16, 128], P(None, 'wall', 'plane')
The draws below stay inside these ranges and needn't reach their ends.
Inputs may be any that keep to these rules, and one draw needn't show every extreme that they name: jacobian[2, :, :, k] is the transpose of jacobian[0, :, :, k + 1], every jacobian[1, :, :, k] is symmetric, and every row of a line's matrix is strictly diagonally dominant with a positive diagonal. `bottom_flag`: 1 where a column's first cell lies on the wake cut, 0 where it lies on the capsule wall. `wake_partner`: for a wake-cut column (i, j), the spanwise index of the column at station (i + 8) modulo 16, on the other branch of the cut, that lies beneath its first cell; each row is a permutation of 0 to 127.
All inputs are finite; a program needn't handle non-finite values. No bound on the sum of `bottom_flag` on one device may be relied on, other than what follows from the above.
Results may differ from the reference program's by a relative error of at most 0.0003.
Values sent between devices are 32-bit elements; how exact they have to be, the bound alone decides.
A program may use at most 192 MiB of HBM per device.

```python
import math
import jax
import jax.numpy as jnp
from jax import lax

NV = 16
NJ = 128
NK = 32
NI = 16


def draw_jacobian(key, part):
    identity = jnp.eye(NV, dtype=jnp.float32)[:, :, None, None, None]
    samples = jax.random.uniform(jax.random.fold_in(key, 1), (NV, NV, NK + 1, NI, NJ), jnp.float32)
    coupling = -(0.6 * identity + 0.1 * samples)
    lower = coupling[:, :, :NK]
    upper = jnp.swapaxes(coupling[:, :, 1:], 0, 1)
    mixing_draw = jax.random.uniform(jax.random.fold_in(key, 2), (NV, NV, NK, NI, NJ), jnp.float32)
    mixing = -0.05 * (mixing_draw + jnp.swapaxes(mixing_draw, 0, 1)) * (1.0 - identity)
    margin = jnp.exp(jax.random.uniform(jax.random.fold_in(key, 3), (NV, NK, NI, NJ), jnp.float32, math.log(0.001), math.log(0.01)))
    total = jnp.sum(jnp.abs(lower), axis=1) + jnp.sum(jnp.abs(upper), axis=1) + jnp.sum(jnp.abs(mixing), axis=1) + margin
    middle = mixing + identity * total[:, None]
    return jnp.stack([lower, middle, upper])


def draw_residual(key, part):
    extent = (NV, NK, NI, NJ)
    return 0.05 * jax.random.normal(jax.random.fold_in(key, 11), extent, jnp.float32)


def plant(array, own_key, least, top_value):
    dims = array.shape
    place = [jax.random.randint(jax.random.fold_in(own_key, axis), (), 0, dims[axis]) for axis in range(len(dims))]
    array = array.at[tuple(place)].set(least)
    longest = dims.index(max(dims))
    place[longest] = (place[longest] + 1) % dims[longest]
    return array.at[tuple(place)].set(top_value)


def level_of(key, shape, split, smallest, largest):
    factor_of = 1.0
    for axis_at, blocks in split:
        draws = jax.random.uniform(jax.random.fold_in(jax.random.fold_in(key, 6), axis_at), (blocks,), jnp.float32, smallest / len(split), largest / len(split))
        factor_of = factor_of * jnp.repeat(jnp.exp(draws), shape[axis_at] // blocks).reshape((-1,) + (1,) * (len(shape) - 1 - axis_at))
    return factor_of


def bell_draw(key, dims, deviation, most, shards=(), kind=jnp.bfloat16):
    drawn = deviation * jax.random.normal(key, dims, jnp.float32)
    if shards:
        drawn = drawn * level_of(key, dims, shards, -0.22, 0.18)
    return jnp.clip(drawn, -most, most).astype(kind)


def setup_inputs(seed: int = 0) -> dict:
    splits = jax.random.split(jax.random.key(seed), 8)
    return {
        "jacobian": draw_jacobian(jax.random.fold_in(splits[7], 71), 0),
        "residual": draw_residual(jax.random.fold_in(splits[7], 71), 0),
        "previous_update": bell_draw(splits[2], (NV, NK, NI, NJ), 1.0, 6.0, ((1, 2), (2, 16)), jnp.float32),
        "offline_coupling": jnp.clip(jnp.exp(math.log(0.03) - 2.3025851 * jax.random.uniform(splits[3], (4, NV, NK, NI, NJ), jnp.float32) ** level_of(splits[3], (4, NV, NK, NI, NJ), ((2, 2), (3, 16)), -0.2, 0.2)), 0.003, 0.03),
        "wake_partner": jax.vmap(lambda own: jax.random.permutation(own, NJ))(jax.random.split(splits[4], NI)).reshape((NI, NJ)).astype(jnp.int32),
        "line_length": plant(jax.random.randint(splits[5], (NI, NJ), NK // 2, NK + 1), jax.random.fold_in(splits[5], 1), NK // 2, NK).astype(jnp.int32),
        "bottom_flag": plant((jax.random.randint(splits[6], (NI, NJ), 0, 2) < 1).astype(jnp.int32), jax.random.fold_in(splits[6], 1), 0, 1),
    }


precise = lax.Precision.HIGHEST


def product(left, right):
    return jnp.einsum("vwc,wuc->vuc", left, right, precision=precise)


def solve_block(matrix, given):
    extent = matrix.shape[0]
    augmented = jnp.concatenate([matrix, given], axis=1)
    for pivot in range(extent):
        pivot_row = augmented[pivot] / augmented[pivot, pivot][None, :]
        augmented = augmented - augmented[:, pivot][:, None, :] * pivot_row[None]
        augmented = augmented.at[pivot].set(pivot_row)
    return augmented[:, extent:]


def effective(lower, middle, upper, active_here, active_above, not_bottom):
    identity = jnp.eye(lower.shape[0], dtype=jnp.float32)[:, :, None, None]
    return (lower * (active_here * not_bottom)[None, None],
            middle * active_here[None, None] + identity * (1.0 - active_here)[None, None],
            upper * active_above[None, None])


def eliminate(lower, middle, upper, source, block_in, vector_in, levels):
    extent = lower.shape[0]
    blocks = jnp.zeros(lower.shape, jnp.float32)
    vectors = jnp.zeros(source.shape, jnp.float32)

    def advance(level, state):
        block_prev, vector_prev, blocks, vectors = state
        below = lax.dynamic_index_in_dim(lower, level, 2, keepdims=False)
        centre = lax.dynamic_index_in_dim(middle, level, 2, keepdims=False)
        above = lax.dynamic_index_in_dim(upper, level, 2, keepdims=False)
        given = lax.dynamic_index_in_dim(source, level, 2, keepdims=False)
        schur = centre - product(below, block_prev)
        reduced = given - product(below, vector_prev)
        joined = solve_block(schur, jnp.concatenate([above, reduced], axis=1))
        block_next = joined[:, :extent]
        vector_next = joined[:, extent:]
        blocks = lax.dynamic_update_index_in_dim(blocks, block_next, level, 2)
        vectors = lax.dynamic_update_index_in_dim(vectors, vector_next, level, 2)
        return block_next, vector_next, blocks, vectors

    return lax.fori_loop(0, levels, advance, (block_in, vector_in, blocks, vectors))


def substitute(blocks, vectors, value_above, levels, result):
    def retreat(count, state):
        value_next, result = state
        level = levels - 1 - count
        block = lax.dynamic_index_in_dim(blocks, level, 2, keepdims=False)
        vector = lax.dynamic_index_in_dim(vectors, level, 2, keepdims=False)
        value = vector - product(block, value_next)
        result = lax.dynamic_update_index_in_dim(result, value, level, 2)
        return value, result

    return lax.fori_loop(0, levels, retreat, (value_above, result))


def reference(jacobian, residual, previous_update, offline_coupling, wake_partner, line_length, bottom_flag):
    padded = jnp.pad(previous_update, ((0, 0), (0, 0), (1, 1), (0, 0)))
    offline = (offline_coupling[0] * padded[:, :, :-2] + offline_coupling[1] * padded[:, :, 2:]
               + offline_coupling[2] * jnp.roll(previous_update, 1, axis=3)
               + offline_coupling[3] * jnp.roll(previous_update, -1, axis=3))
    mirrored = jnp.roll(previous_update[:, 0], NI // 2, axis=1)
    partner = jnp.take_along_axis(mirrored, wake_partner.astype(jnp.int32)[None], axis=2)
    wake = jnp.einsum("vwij,wij->vij", jacobian[0, :, :, 0], partner, precision=precise)
    wake = wake * bottom_flag.astype(jnp.float32)[None]
    levels = jnp.arange(NK, dtype=jnp.int32)
    active = (levels[:, None, None] < line_length[None]).astype(jnp.float32)
    active_above = ((levels + 1)[:, None, None] < line_length[None]).astype(jnp.float32)
    not_bottom = (levels > 0).astype(jnp.float32)[:, None]
    source = residual + offline
    source = source.at[:, 0].add(-wake)
    source = source * active[None]

    def station(index):
        blocks = lax.dynamic_index_in_dim(jacobian, index, 4, keepdims=False)
        here = lax.dynamic_index_in_dim(active, index, 1, keepdims=False)
        above = lax.dynamic_index_in_dim(active_above, index, 1, keepdims=False)
        given = lax.dynamic_index_in_dim(source, index, 2, keepdims=False)[:, None]
        lower, middle, upper = effective(blocks[0], blocks[1], blocks[2], here, above, not_bottom)
        empty_block = jnp.zeros((NV, NV, NJ), jnp.float32)
        empty_vector = jnp.zeros((NV, 1, NJ), jnp.float32)
        parts = eliminate(lower, middle, upper, given, empty_block, empty_vector, NK)
        solved = substitute(parts[2], parts[3], empty_vector, NK, jnp.zeros(given.shape, jnp.float32))
        return solved[1][:, 0]

    stacked = lax.map(station, jnp.arange(NI, dtype=jnp.int32))
    return jnp.moveaxis(stacked, 0, 2)
```

```python
import functools

import jax
import jax.numpy as jnp
from jax import lax
from jax.experimental import pallas as pl
from jax.experimental.pallas import tpu as pltpu
from jax.sharding import PartitionSpec as P

MESH = pl.DeviceIdType.MESH


def spread(row, index, rows):
    return jnp.broadcast_to(row[index : index + 1, :], (rows, row.shape[1]))


def sweep(low, high, right):
    extent = len(low)
    half = low[0].shape[0]
    place = lax.broadcasted_iota(jnp.int32, low[0].shape, 0)
    for pivot in range(extent):
        in_low = pivot < half
        at = pivot % half
        pivot_low, pivot_high = low[pivot], high[pivot]
        inverse = 1.0 / spread(pivot_low if in_low else pivot_high, at, half)
        here = place == at
        scaled_low, scaled_high = pivot_low * inverse, pivot_high * inverse
        if in_low:
            scaled_low = jnp.where(here, -inverse, scaled_low)
        else:
            scaled_high = jnp.where(here, -inverse, scaled_high)
        if right is not None:
            scaled_right = tuple(part * inverse for part in right[pivot])
        order = [(pivot + 1 + step) % extent for step in range(extent - 1)]
        for row in order:
            factor = spread(pivot_low if row < half else pivot_high, row % half, half)
            kept_low, kept_high = low[row], high[row]
            if in_low:
                kept_low = jnp.where(here, 0.0, kept_low)
            else:
                kept_high = jnp.where(here, 0.0, kept_high)
            low[row] = kept_low - factor * scaled_low
            high[row] = kept_high - factor * scaled_high
            if right is not None:
                right[row] = tuple(
                    part - factor * scaled for part, scaled in zip(right[row], scaled_right)
                )
        low[pivot], high[pivot] = scaled_low, scaled_high
        if right is not None:
            right[pivot] = scaled_right


def total(terms):
    while len(terms) > 1:
        terms = [
            terms[at] + terms[at + 1] if at + 1 < len(terms) else terms[at]
            for at in range(0, len(terms), 2)
        ]
    return terms[0]


def kernel(
    extent,
    depth,
    jacobian,
    residual,
    previous,
    coupling,
    partner_map,
    length,
    flag,
    out,
    near,
    centre,
    first,
    schur,
    inverse,
    carry,
    masked,
    source,
    reduced,
    fixed,
    bottom,
    facing,
    from_left,
    from_right,
    block_out,
    block_in,
    vector_out,
    vector_in,
    copy_sems,
    send_sems,
    recv_sems,
):
    wall = lax.axis_index("wall")
    plane = lax.axis_index("plane")
    planes = lax.axis_size("plane")
    half = extent // 2
    right = {"wall": wall, "plane": lax.rem(plane + 1, planes)}
    left = {"wall": wall, "plane": lax.rem(plane + planes - 1, planes)}
    mirror = {"wall": wall, "plane": lax.rem(plane + planes // 2, planes)}
    across = {"wall": 1 - wall, "plane": plane}

    fetch_centre = pltpu.make_async_copy(jacobian.at[1], centre, copy_sems.at[0])
    fetch_near = pltpu.make_async_copy(jacobian.at[2 - 2 * wall], near, copy_sems.at[1])
    fetch_first = pltpu.make_async_copy(jacobian.at[0], first, copy_sems.at[2])
    fetch_centre.start()
    fetch_near.start()
    fetch_first.start()

    bottom[...] = previous[pl.ds(0, extent, stride=depth), :]
    barrier = pltpu.get_barrier_semaphore()
    for device in (right, left, mirror, across):
        pl.semaphore_signal(barrier, inc=1, device_id=device, device_id_type=MESH)
    pl.semaphore_wait(barrier, 4)

    def send(origin, target, number, device):
        return pltpu.make_async_remote_copy(
            src_ref=origin,
            dst_ref=target,
            send_sem=send_sems.at[number],
            recv_sem=recv_sems.at[number],
            device_id=device,
            device_id_type=MESH,
        )

    to_right = send(previous, from_left, 0, right)
    to_left = send(previous, from_right, 1, left)
    to_mirror = send(bottom, facing, 2, mirror)
    to_right.start()
    to_left.start()
    to_mirror.start()

    lengths = length[...]
    base = wall * depth

    def level_at(step):
        return step + wall * (depth - 1 - 2 * step)

    def mask_at(level):
        return jnp.where(level < lengths, 1.0, 0.0).astype(jnp.float32)

    place = lax.broadcasted_iota(jnp.int32, (extent, lengths.shape[1]), 0)

    def diagonal(step, row):
        level = level_at(step)
        mask = mask_at(level + base)
        block = centre[pl.ds(row * extent * depth + level, extent, stride=depth), :]
        return block * mask + jnp.where(place == row, 1.0 - mask, 0.0)

    fetch_centre.wait()
    for row in range(extent):
        schur[pl.ds(row * extent, extent), :] = diagonal(0, row)
    fetch_near.wait()

    def advance(step, _):
        level = level_at(step)
        start = pl.multiple_of(step * (extent * extent), extent * extent)
        mask = mask_at(level + base + 1 - wall)
        low, high, beyond = [], [], []
        for row in range(extent):
            low.append(schur[pl.ds(start + row * extent, half), :])
            high.append(schur[pl.ds(start + row * extent + half, half), :])
            block = near[pl.ds(row * extent * depth + level, extent, stride=depth), :] * mask
            masked[row * extent : (row + 1) * extent, :] = block
            beyond.append((block[:half], block[half:]))
        sweep(low, high, beyond)
        for row in range(extent):
            inverse[pl.ds(start + row * extent, half), :] = low[row]
            inverse[pl.ds(start + row * extent + half, half), :] = high[row]
            carry[pl.ds(start + row * extent, half), :] = beyond[row][0]
            carry[pl.ds(start + row * extent + half, half), :] = beyond[row][1]
        following = jnp.minimum(step + 1, depth - 1)
        ahead = pl.multiple_of((step + 1) * (extent * extent), extent * extent)
        for row in range(extent):
            change_low, change_high = None, None
            for inner in range(extent):
                factor = jnp.broadcast_to(
                    masked[inner * extent + row : inner * extent + row + 1, :],
                    (half, lengths.shape[1]),
                )
                term_low, term_high = factor * beyond[inner][0], factor * beyond[inner][1]
                change_low = term_low if inner == 0 else change_low + term_low
                change_high = term_high if inner == 0 else change_high + term_high
            block_out[row * extent : row * extent + half, :] = change_low
            block_out[row * extent + half : (row + 1) * extent, :] = change_high
            block = diagonal(following, row)
            schur[pl.ds(ahead + row * extent, half), :] = block[:half] - change_low
            schur[pl.ds(ahead + row * extent + half, half), :] = block[half:] - change_high
        return 0

    lax.fori_loop(0, depth, advance, 0)
    to_across = send(block_out, block_in, 3, across)
    to_across.start()

    fetch_first.wait()
    to_right.wait()
    to_left.wait()
    to_mirror.wait()
    own = previous[...]
    has_left = jnp.where(plane > 0, 1.0, 0.0).astype(jnp.float32)
    has_right = jnp.where(plane < planes - 1, 1.0, 0.0).astype(jnp.float32)
    span = lengths.shape[1]
    offline = (
        coupling[0] * (from_left[...] * has_left)
        + coupling[1] * (from_right[...] * has_right)
        + coupling[2] * pltpu.roll(own, 1, 1)
        + coupling[3] * pltpu.roll(own, span - 1, 1)
    )
    rows = extent * depth
    levels = lax.rem(lax.broadcasted_iota(jnp.int32, (rows, span), 0), depth) + base
    active = jnp.where(levels < lengths, 1.0, 0.0).astype(jnp.float32)
    source[...] = (residual[...] + offline) * active
    chosen = jnp.where(
        lax.broadcasted_iota(jnp.int32, (span, span), 0) == partner_map[...], 1.0, 0.0
    ).astype(jnp.float32)
    partner = jnp.dot(
        facing[...], chosen, precision=lax.Precision.HIGHEST, preferred_element_type=jnp.float32
    )
    wake = total(
        [
            first[pl.ds(inner * depth, extent, stride=extent * depth), :]
            * spread(partner, inner, extent)
            for inner in range(extent)
        ]
    )
    weight = flag[...].astype(jnp.float32) * jnp.where(wall == 0, 1.0, 0.0).astype(jnp.float32)
    bottom_rows = pl.ds(0, extent, stride=depth)
    source[bottom_rows, :] = source[bottom_rows, :] - wake * weight * mask_at(base)

    def source_at(step):
        return source[pl.ds(level_at(step), extent, stride=depth), :]

    reduced[0:extent, :] = source_at(0)

    def forward(step, vector):
        start = pl.multiple_of(step * (extent * extent), extent * extent)
        spreads = [spread(vector, row, extent) for row in range(extent)]
        change = total(
            [spreads[row] * carry[pl.ds(start + row * extent, extent), :] for row in range(extent)]
        )
        given = total(
            [spreads[row] * inverse[pl.ds(start + row * extent, extent), :] for row in range(extent)]
        )
        fixed[pl.ds(pl.multiple_of(step * extent, extent), extent), :] = -given
        vector_out[...] = change
        following = source_at(jnp.minimum(step + 1, depth - 1)) - change
        reduced[pl.ds(pl.multiple_of((step + 1) * extent, extent), extent), :] = following
        return following

    lax.fori_loop(0, depth, forward, source_at(0))
    vector_across = send(vector_out, vector_in, 4, across)
    vector_across.start()

    to_across.wait()
    last = (depth - 1) * extent * extent
    low, high = [], []
    for row in range(extent):
        here = last + row * extent
        low.append(schur[here : here + half, :] - block_in[row * extent : row * extent + half, :])
        high.append(
            schur[here + half : here + extent, :]
            - block_in[row * extent + half : (row + 1) * extent, :]
        )
    sweep(low, high, None)
    vector_across.wait()
    given = reduced[(depth - 1) * extent : depth * extent, :] - vector_in[...]
    spreads = [spread(given, row, half) for row in range(extent)]
    value = -jnp.concatenate(
        [
            total([spreads[row] * low[row] for row in range(extent)]),
            total([spreads[row] * high[row] for row in range(extent)]),
        ],
        axis=0,
    )
    out[pl.ds(level_at(depth - 1), extent, stride=depth), :] = value

    def backward(count, value):
        step = depth - 2 - count
        start = pl.multiple_of(step * (extent * extent), extent * extent)
        change = total(
            [
                spread(value, column, extent)
                * carry[pl.ds(start + column, extent, stride=extent), :]
                for column in range(extent)
            ]
        )
        value = fixed[pl.ds(pl.multiple_of(step * extent, extent), extent), :] - change
        out[pl.ds(level_at(step), extent, stride=depth), :] = value
        return value

    lax.fori_loop(0, depth - 1, backward, value)


def per_device(
    jacobian, residual, previous_update, offline_coupling, wake_partner, line_length, bottom_flag
):
    extent, depth, span = jacobian.shape[1], jacobian.shape[3], jacobian.shape[5]
    block = extent * extent
    whole = pl.BlockSpec(memory_space=pltpu.VMEM)
    f32 = jnp.float32

    def room(rows):
        return pltpu.VMEM((rows, span), f32)

    result = pl.pallas_call(
        functools.partial(kernel, extent, depth),
        out_shape=jax.ShapeDtypeStruct((extent * depth, span), f32),
        in_specs=[pl.BlockSpec(memory_space=pl.ANY)] + [whole] * 6,
        out_specs=whole,
        scratch_shapes=[
            room(block * depth),
            room(block * depth),
            room(block * depth),
            room(block * (depth + 1)),
            room(block * depth),
            room(block * depth),
            room(block),
            room(extent * depth),
            room(extent * (depth + 1)),
            room(extent * depth),
            room(extent),
            room(extent),
            room(extent * depth),
            room(extent * depth),
            room(block),
            room(block),
            room(extent),
            room(extent),
            pltpu.SemaphoreType.DMA((3,)),
            pltpu.SemaphoreType.DMA((5,)),
            pltpu.SemaphoreType.DMA((5,)),
        ],
        compiler_params=pltpu.CompilerParams(
            collective_id=0, has_side_effects=True, vmem_limit_bytes=40 * 1024 * 1024
        ),
    )(
        jacobian.reshape(3, block * depth, span),
        residual.reshape(extent * depth, span),
        previous_update.reshape(extent * depth, span),
        offline_coupling.reshape(4, extent * depth, span),
        wake_partner,
        line_length,
        bottom_flag,
    )
    return result.reshape(extent, depth, 1, span)


def solution(mesh):
    return jax.shard_map(
        per_device,
        mesh=mesh,
        in_specs=(
            P(None, None, None, "wall", "plane", None),
            P(None, "wall", "plane", None),
            P(None, "wall", "plane", None),
            P(None, None, "wall", "plane", None),
            P("plane", None),
            P("plane", None),
            P("plane", None),
        ),
        out_specs=P(None, "wall", "plane", None),
        check_vma=False,
    )
```

```python
import functools

import jax
import jax.numpy as jnp
from jax import lax
from jax.experimental import pallas as pl
from jax.experimental.pallas import tpu as pltpu
from jax.sharding import PartitionSpec as P

MESH = pl.DeviceIdType.MESH


def spread(row, index, rows):
    return jnp.broadcast_to(row[index : index + 1, :], (rows, row.shape[1]))


def sweep(low, high, right, following):
    extent = len(low)
    half = low[0].shape[0]
    group = 4
    place = lax.broadcasted_iota(jnp.int32, low[0].shape, 0)

    def entry(row, column):
        return spread(low[row] if column < half else high[row], column % half, half)

    inverse = 1.0 / entry(0, 0)
    finished = []
    for pivot in range(extent):
        in_low = pivot < half
        here = place == pivot % half
        pivot_low, pivot_high = low[pivot], high[pivot]
        if pivot + 1 < extent:
            beside = entry(pivot, pivot + 1)
            next_inverse = 1.0 / (entry(pivot + 1, pivot + 1) - beside * (beside * inverse))
        scaled_low, scaled_high = pivot_low * inverse, pivot_high * inverse
        if in_low:
            scaled_low = jnp.where(here, -inverse, scaled_low)
        else:
            scaled_high = jnp.where(here, -inverse, scaled_high)
        if right is not None:
            scaled_right = tuple(part * inverse for part in right[pivot])
            finished.append((right[pivot], scaled_right))
        order = [(pivot + 1 + step) % extent for step in range(extent - 1)]
        for row in order:
            factor = spread(pivot_low if row < half else pivot_high, row % half, half)
            kept_low, kept_high = low[row], high[row]
            if in_low:
                kept_low = jnp.where(here, 0.0, kept_low)
            else:
                kept_high = jnp.where(here, 0.0, kept_high)
            low[row] = kept_low - factor * scaled_low
            high[row] = kept_high - factor * scaled_high
            if right is not None:
                right[row] = tuple(
                    part - factor * scaled for part, scaled in zip(right[row], scaled_right)
                )
        low[pivot], high[pivot] = scaled_low, scaled_high
        if right is not None:
            right[pivot] = scaled_right
        if len(finished) == group:
            next_low, next_high = following
            for row in range(extent):
                factors = [
                    spread(plain[row // half], row % half, half) for plain, _ in finished
                ]
                if row < half:
                    next_low[row] = next_low[row] - total(
                        [factor * scaled[0] for factor, (_, scaled) in zip(factors, finished)]
                    )
                next_high[row] = next_high[row] - total(
                    [factor * scaled[1] for factor, (_, scaled) in zip(factors, finished)]
                )
            finished = []
        inverse = next_inverse


def total(terms):
    while len(terms) > 1:
        terms = [
            terms[at] + terms[at + 1] if at + 1 < len(terms) else terms[at]
            for at in range(0, len(terms), 2)
        ]
    return terms[0]


def kernel(
    extent,
    depth,
    jacobian,
    residual_far,
    previous_far,
    coupling_far,
    partner_far,
    length_far,
    flag_far,
    out,
    residual,
    previous,
    coupling,
    partner_map,
    length,
    flag,
    near_store,
    centre_store,
    first,
    schur,
    inverse,
    carry,
    source,
    reduced,
    fixed,
    bottom,
    facing,
    from_left,
    from_right,
    block_out,
    block_in,
    vector_out,
    vector_in,
    copy_sems,
    send_sems,
    recv_sems,
):
    wall = lax.axis_index("wall")
    plane = lax.axis_index("plane")
    planes = lax.axis_size("plane")
    half = extent // 2
    right = {"wall": wall, "plane": lax.rem(plane + 1, planes)}
    left = {"wall": wall, "plane": lax.rem(plane + planes - 1, planes)}
    mirror = {"wall": wall, "plane": lax.rem(plane + planes // 2, planes)}
    across = {"wall": 1 - wall, "plane": plane}

    near = near_store.reshape(extent * extent * depth, near_store.shape[2])
    centre = centre_store.reshape(extent * extent * depth, near_store.shape[2])
    middle = depth // 2
    halves = [pl.multiple_of(wall * middle, middle), pl.multiple_of((1 - wall) * middle, middle)]
    near_at = 2 - 2 * wall
    fetches = [
        pltpu.make_async_copy(previous_far, previous, copy_sems.at[0]),
        pltpu.make_async_copy(length_far, length, copy_sems.at[1]),
    ]
    for at, part in enumerate(halves):
        levels_here = pl.ds(part, middle)
        fetches.append(
            pltpu.make_async_copy(
                jacobian.at[1, :, levels_here], centre_store.at[:, levels_here], copy_sems.at[2 + 2 * at]
            )
        )
        fetches.append(
            pltpu.make_async_copy(
                jacobian.at[near_at, :, levels_here],
                near_store.at[:, levels_here],
                copy_sems.at[3 + 2 * at],
            )
        )
    late = [
        pltpu.make_async_copy(jacobian.at[0, :, pl.ds(0, middle)], first, copy_sems.at[6]),
        pltpu.make_async_copy(residual_far, residual, copy_sems.at[7]),
        pltpu.make_async_copy(coupling_far, coupling, copy_sems.at[8]),
        pltpu.make_async_copy(partner_far, partner_map, copy_sems.at[9]),
        pltpu.make_async_copy(flag_far, flag, copy_sems.at[10]),
    ]
    for fetch in fetches + late:
        fetch.start()
    fetches[0].wait()
    fetches[1].wait()

    bottom[...] = previous[pl.ds(0, extent, stride=depth), :]
    barrier = pltpu.get_barrier_semaphore()
    for device in (right, left, mirror, across):
        pl.semaphore_signal(barrier, inc=1, device_id=device, device_id_type=MESH)
    pl.semaphore_wait(barrier, 4)

    def send(origin, target, number, device):
        return pltpu.make_async_remote_copy(
            src_ref=origin,
            dst_ref=target,
            send_sem=send_sems.at[number],
            recv_sem=recv_sems.at[number],
            device_id=device,
            device_id_type=MESH,
        )

    to_right = send(previous, from_left, 0, right)
    to_left = send(previous, from_right, 1, left)
    to_mirror = send(bottom, facing, 2, mirror)
    to_right.start()
    to_left.start()
    to_mirror.start()

    lengths = length[...]
    base = wall * depth

    def level_at(step):
        return step + wall * (depth - 1 - 2 * step)

    def mask_at(level):
        return jnp.where(level < lengths, 1.0, 0.0).astype(jnp.float32)

    place = lax.broadcasted_iota(jnp.int32, (extent, lengths.shape[1]), 0)

    def diagonal(step, row):
        level = level_at(step)
        mask = mask_at(level + base)
        block = centre[pl.ds(row * extent * depth + level, extent, stride=depth), :]
        return block * mask + jnp.where(place == row, 1.0 - mask, 0.0)

    fetches[2].wait()
    for row in range(extent):
        schur[pl.ds(row * extent, extent), :] = diagonal(0, row)
    fetches[3].wait()

    def advance(step, _):
        level = level_at(step)
        start = pl.multiple_of(step * (extent * extent), extent * extent)
        mask = mask_at(level + base + 1 - wall)
        low, high, beyond = [], [], []
        next_low, next_high = [], []
        following = jnp.minimum(step + 1, depth - 1)
        kept = jnp.where(step < depth - 1, 1.0, 0.0).astype(jnp.float32)
        for row in range(extent):
            if row < half:
                low.append(schur[pl.ds(start + row * extent, half), :])
            else:
                low.append(schur[pl.ds(start + row, half, stride=extent), :])
            high.append(schur[pl.ds(start + row * extent + half, half), :])
            block = near[pl.ds(row * extent * depth + level, extent, stride=depth), :] * mask
            beyond.append((block[:half], block[half:]))
            block = diagonal(following, row) * kept
            next_low.append(block[:half])
            next_high.append(block[half:])
        sweep(low, high, beyond, (next_low, next_high))
        ahead = pl.multiple_of((step + 1) * (extent * extent), extent * extent)
        for row in range(extent):
            inverse[pl.ds(start + row * extent, half), :] = low[row]
            inverse[pl.ds(start + row * extent + half, half), :] = high[row]
            carry[pl.ds(start + row * extent, half), :] = beyond[row][0]
            carry[pl.ds(start + row * extent + half, half), :] = beyond[row][1]
            if row < half:
                schur[pl.ds(ahead + row * extent, half), :] = next_low[row]
            schur[pl.ds(ahead + row * extent + half, half), :] = next_high[row]
        return 0

    lax.fori_loop(0, middle - 1, advance, 0)
    fetches[4].wait()
    fetches[5].wait()
    lax.fori_loop(middle - 1, depth, advance, 0)
    done = depth * extent * extent
    upper = half * extent
    block_out[0:upper, :] = schur[done : done + upper, :]
    for row in range(half):
        here = done + (half + row) * extent + half
        block_out[upper + row * half : upper + (row + 1) * half, :] = schur[here : here + half, :]
    to_across = send(block_out, block_in, 3, across)
    to_across.start()

    for fetch in late:
        fetch.wait()
    to_right.wait()
    to_left.wait()
    to_mirror.wait()
    own = previous[...]
    has_left = jnp.where(plane > 0, 1.0, 0.0).astype(jnp.float32)
    has_right = jnp.where(plane < planes - 1, 1.0, 0.0).astype(jnp.float32)
    span = lengths.shape[1]
    offline = (
        coupling[0] * (from_left[...] * has_left)
        + coupling[1] * (from_right[...] * has_right)
        + coupling[2] * pltpu.roll(own, 1, 1)
        + coupling[3] * pltpu.roll(own, span - 1, 1)
    )
    rows = extent * depth
    levels = lax.rem(lax.broadcasted_iota(jnp.int32, (rows, span), 0), depth) + base
    active = jnp.where(levels < lengths, 1.0, 0.0).astype(jnp.float32)
    source[...] = (residual[...] + offline) * active
    chosen = jnp.where(
        lax.broadcasted_iota(jnp.int32, (span, span), 0) == partner_map[...], 1.0, 0.0
    ).astype(jnp.float32)
    partner = jnp.dot(
        facing[...], chosen, precision=lax.Precision.HIGHEST, preferred_element_type=jnp.float32
    )
    first_rows = first.reshape(extent * extent * middle, span)
    wake = total(
        [
            first_rows[pl.ds(inner * middle, extent, stride=extent * middle), :]
            * spread(partner, inner, extent)
            for inner in range(extent)
        ]
    )
    weight = flag[...].astype(jnp.float32) * jnp.where(wall == 0, 1.0, 0.0).astype(jnp.float32)
    bottom_rows = pl.ds(0, extent, stride=depth)
    source[bottom_rows, :] = source[bottom_rows, :] - wake * weight * mask_at(base)

    def source_at(step):
        return source[pl.ds(level_at(step), extent, stride=depth), :]

    reduced[0:extent, :] = source_at(0)

    def forward(step, vector):
        start = pl.multiple_of(step * (extent * extent), extent * extent)
        spreads = [spread(vector, row, extent) for row in range(extent)]
        change = total(
            [spreads[row] * carry[pl.ds(start + row * extent, extent), :] for row in range(extent)]
        )
        given = total(
            [spreads[row] * inverse[pl.ds(start + row * extent, extent), :] for row in range(extent)]
        )
        fixed[pl.ds(pl.multiple_of(step * extent, extent), extent), :] = -given
        vector_out[...] = change
        following = source_at(jnp.minimum(step + 1, depth - 1)) - change
        reduced[pl.ds(pl.multiple_of((step + 1) * extent, extent), extent), :] = following
        return following

    lax.fori_loop(0, depth, forward, source_at(0))
    vector_across = send(vector_out, vector_in, 4, across)
    vector_across.start()

    to_across.wait()
    last = (depth - 1) * extent * extent
    low, high = [], []
    for row in range(extent):
        here = last + row * extent
        if row < half:
            low.append(schur[here : here + half, :] + block_in[row * extent : row * extent + half, :])
            high.append(
                schur[here + half : here + extent, :]
                + block_in[row * extent + half : (row + 1) * extent, :]
            )
        else:
            low.append(
                schur[pl.ds(last + row, half, stride=extent), :]
                + block_in[pl.ds(row, half, stride=extent), :]
            )
            at = upper + (row - half) * half
            high.append(schur[here + half : here + extent, :] + block_in[at : at + half, :])
    sweep(low, high, None, None)
    vector_across.wait()
    given = reduced[(depth - 1) * extent : depth * extent, :] - vector_in[...]
    spreads = [spread(given, row, half) for row in range(extent)]
    value = -jnp.concatenate(
        [
            total([spreads[row] * low[row] for row in range(extent)]),
            total([spreads[row] * high[row] for row in range(extent)]),
        ],
        axis=0,
    )
    out[pl.ds(level_at(depth - 1), extent, stride=depth), :] = value

    def backward(count, value):
        step = depth - 2 - count
        start = pl.multiple_of(step * (extent * extent), extent * extent)
        change = total(
            [
                spread(value, column, extent)
                * carry[pl.ds(start + column, extent, stride=extent), :]
                for column in range(extent)
            ]
        )
        value = fixed[pl.ds(pl.multiple_of(step * extent, extent), extent), :] - change
        out[pl.ds(level_at(step), extent, stride=depth), :] = value
        return value

    lax.fori_loop(0, depth - 1, backward, value)


def per_device(
    jacobian, residual, previous_update, offline_coupling, wake_partner, line_length, bottom_flag
):
    extent, depth, span = jacobian.shape[1], jacobian.shape[3], jacobian.shape[5]
    block = extent * extent
    whole = pl.BlockSpec(memory_space=pltpu.VMEM)
    f32 = jnp.float32

    def room(rows):
        return pltpu.VMEM((rows, span), f32)

    result = pl.pallas_call(
        functools.partial(kernel, extent, depth),
        out_shape=jax.ShapeDtypeStruct((extent * depth, span), f32),
        in_specs=[pl.BlockSpec(memory_space=pl.ANY)] * 7,
        out_specs=whole,
        scratch_shapes=[
            room(extent * depth),
            room(extent * depth),
            pltpu.VMEM((4, extent * depth, span), f32),
            pltpu.VMEM((1, span), jnp.int32),
            pltpu.VMEM((1, span), jnp.int32),
            pltpu.VMEM((1, span), jnp.int32),
            pltpu.VMEM((block, depth, span), f32),
            pltpu.VMEM((block, depth, span), f32),
            pltpu.VMEM((block, depth // 2, span), f32),
            room(block * (depth + 1)),
            room(block * depth),
            room(block * depth),
            room(extent * depth),
            room(extent * (depth + 1)),
            room(extent * depth),
            room(extent),
            room(extent),
            room(extent * depth),
            room(extent * depth),
            room(block * 3 // 4),
            room(block * 3 // 4),
            room(extent),
            room(extent),
            pltpu.SemaphoreType.DMA((11,)),
            pltpu.SemaphoreType.DMA((5,)),
            pltpu.SemaphoreType.DMA((5,)),
        ],
        compiler_params=pltpu.CompilerParams(
            collective_id=0, has_side_effects=True, vmem_limit_bytes=63 * 1024 * 1024
        ),
    )(
        jacobian.reshape(3, block, depth, span),
        residual.reshape(extent * depth, span),
        previous_update.reshape(extent * depth, span),
        offline_coupling.reshape(4, extent * depth, span),
        wake_partner,
        line_length,
        bottom_flag,
    )
    return result.reshape(extent, depth, 1, span)


def solution(mesh):
    return jax.shard_map(
        per_device,
        mesh=mesh,
        in_specs=(
            P(None, None, None, "wall", "plane", None),
            P(None, "wall", "plane", None),
            P(None, "wall", "plane", None),
            P(None, None, "wall", "plane", None),
            P("plane", None),
            P("plane", None),
            P("plane", None),
        ),
        out_specs=P(None, "wall", "plane", None),
        check_vma=False,
    )
```

```python
import functools

import jax
import jax.numpy as jnp
from jax import lax
from jax.experimental import pallas as pl
from jax.experimental.pallas import tpu as pltpu
from jax.sharding import PartitionSpec as P

MESH = pl.DeviceIdType.MESH


def spread(row, index, rows):
    return jnp.broadcast_to(row[index : index + 1, :], (rows, row.shape[1]))


def factor(low, high, right, following):
    extent = len(high)
    half = high[0].shape[0]
    group = 4
    place = lax.broadcasted_iota(jnp.int32, high[0].shape, 0)
    scales = [jnp.zeros_like(high[0]), jnp.zeros_like(high[0])]

    def entry(row, column):
        return spread(low[row] if column < half else high[row], column % half, half)

    inverse = 1.0 / entry(0, 0)
    finished = []
    for pivot in range(extent):
        in_low = pivot < half
        at = pivot % half
        here = place == at
        pivot_low, pivot_high = low[pivot], high[pivot]
        if pivot + 1 < extent:
            beside = entry(pivot, pivot + 1)
            next_inverse = 1.0 / (entry(pivot + 1, pivot + 1) - beside * (beside * inverse))
        scales[pivot // half] = jnp.where(here, inverse, scales[pivot // half])
        scaled_low, scaled_high = pivot_low * inverse, pivot_high * inverse
        if in_low:
            scaled_low = jnp.where(here, inverse, scaled_low)
            known_low = jnp.where(place <= at, scaled_low, 0.0)
            low[pivot] = jnp.where(place < at, pivot_low, jnp.where(here, 1.0, 0.0))
            high[pivot] = None
        else:
            scaled_high = jnp.where(here, inverse, scaled_high)
            high[pivot] = jnp.where(place < at, pivot_high, jnp.where(here, 1.0, 0.0))
        if right is not None:
            scaled_right = tuple(part * inverse for part in right[pivot])
            finished.append((right[pivot], scaled_right))
            right[pivot] = scaled_right
        for row in range(pivot + 1, extent):
            by = spread(pivot_low if row < half else pivot_high, row % half, half)
            if row < half:
                low[row] = jnp.where(here, 0.0, low[row]) - by * scaled_low
                high[row] = high[row] - by * scaled_high
            elif in_low:
                low[row] = -(by * known_low) if pivot == 0 else low[row] - by * known_low
                high[row] = high[row] - by * scaled_high
            else:
                low[row] = low[row] - by * scaled_low
                high[row] = jnp.where(here, 0.0, high[row]) - by * scaled_high
            if right is not None:
                right[row] = tuple(
                    part - by * scaled for part, scaled in zip(right[row], scaled_right)
                )
        if len(finished) == group:
            next_low, next_high = following
            for row in range(extent):
                bys = [spread(plain[row // half], row % half, half) for plain, _ in finished]
                if row < half:
                    next_low[row] = next_low[row] - total(
                        [by * scaled[0] for by, (_, scaled) in zip(bys, finished)]
                    )
                next_high[row] = next_high[row] - total(
                    [by * scaled[1] for by, (_, scaled) in zip(bys, finished)]
                )
            finished = []
        inverse = next_inverse
    return scales


def total(terms):
    while len(terms) > 1:
        terms = [
            terms[at] + terms[at + 1] if at + 1 < len(terms) else terms[at]
            for at in range(0, len(terms), 2)
        ]
    return terms[0]


def kernel(
    extent,
    depth,
    jacobian,
    residual_far,
    previous_far,
    coupling_far,
    partner_far,
    length_far,
    flag_far,
    out,
    residual,
    previous,
    coupling,
    partner_map,
    length,
    flag,
    near_store,
    centre_store,
    first,
    schur,
    inverse,
    carry,
    source,
    reduced,
    fixed,
    scale,
    bottom,
    facing,
    from_left,
    from_right,
    block_out,
    block_in,
    vector_out,
    vector_in,
    copy_sems,
    send_sems,
    recv_sems,
):
    wall = lax.axis_index("wall")
    plane = lax.axis_index("plane")
    planes = lax.axis_size("plane")
    half = extent // 2
    right = {"wall": wall, "plane": lax.rem(plane + 1, planes)}
    left = {"wall": wall, "plane": lax.rem(plane + planes - 1, planes)}
    mirror = {"wall": wall, "plane": lax.rem(plane + planes // 2, planes)}
    across = {"wall": 1 - wall, "plane": plane}

    near = near_store.reshape(extent * extent * depth, near_store.shape[2])
    centre = centre_store.reshape(extent * extent * depth, near_store.shape[2])
    middle = depth // 2
    halves = [pl.multiple_of(wall * middle, middle), pl.multiple_of((1 - wall) * middle, middle)]
    near_at = 2 - 2 * wall
    fetches = [
        pltpu.make_async_copy(previous_far, previous, copy_sems.at[0]),
        pltpu.make_async_copy(length_far, length, copy_sems.at[1]),
    ]
    for at, part in enumerate(halves):
        levels_here = pl.ds(part, middle)
        fetches.append(
            pltpu.make_async_copy(
                jacobian.at[1, :, levels_here], centre_store.at[:, levels_here], copy_sems.at[2 + 2 * at]
            )
        )
        fetches.append(
            pltpu.make_async_copy(
                jacobian.at[near_at, :, levels_here],
                near_store.at[:, levels_here],
                copy_sems.at[3 + 2 * at],
            )
        )
    late = [
        pltpu.make_async_copy(jacobian.at[0, :, pl.ds(0, middle)], first, copy_sems.at[6]),
        pltpu.make_async_copy(residual_far, residual, copy_sems.at[7]),
        pltpu.make_async_copy(coupling_far, coupling, copy_sems.at[8]),
        pltpu.make_async_copy(partner_far, partner_map, copy_sems.at[9]),
        pltpu.make_async_copy(flag_far, flag, copy_sems.at[10]),
    ]
    for fetch in fetches + late:
        fetch.start()
    fetches[0].wait()
    fetches[1].wait()

    bottom[...] = previous[pl.ds(0, extent, stride=depth), :]
    barrier = pltpu.get_barrier_semaphore()
    for device in (right, left, mirror, across):
        pl.semaphore_signal(barrier, inc=1, device_id=device, device_id_type=MESH)
    lengths = length[...]
    base = wall * depth

    def level_at(step):
        return step + wall * (depth - 1 - 2 * step)

    def mask_at(level):
        return jnp.where(level < lengths, 1.0, 0.0).astype(jnp.float32)

    place = lax.broadcasted_iota(jnp.int32, (extent, lengths.shape[1]), 0)

    def diagonal(step, row):
        level = level_at(step)
        mask = mask_at(level + base)
        block = centre[pl.ds(row * extent * depth + level, extent, stride=depth), :]
        return block * mask + jnp.where(place == row, 1.0 - mask, 0.0)

    fetches[2].wait()
    for row in range(extent):
        schur[pl.ds(row * extent, extent), :] = diagonal(0, row)
    fetches[3].wait()

    def advance(step, _):
        level = level_at(step)
        start = pl.multiple_of(step * (extent * extent), extent * extent)
        mask = mask_at(level + base + 1 - wall)
        low, high, beyond = [], [], []
        next_low, next_high = [], []
        following = jnp.minimum(step + 1, depth - 1)
        kept = jnp.where(step < depth - 1, 1.0, 0.0).astype(jnp.float32)
        for row in range(extent):
            low.append(schur[pl.ds(start + row * extent, half), :] if row < half else None)
            high.append(schur[pl.ds(start + row * extent + half, half), :])
            block = near[pl.ds(row * extent * depth + level, extent, stride=depth), :] * mask
            beyond.append((block[:half], block[half:]))
            block = diagonal(following, row) * kept
            next_low.append(block[:half])
            next_high.append(block[half:])
        scales = factor(low, high, beyond, (next_low, next_high))
        ahead = pl.multiple_of((step + 1) * (extent * extent), extent * extent)
        scale_at = pl.multiple_of(step * extent, extent)
        scale[pl.ds(scale_at, half), :] = scales[0]
        scale[pl.ds(scale_at + half, half), :] = scales[1]
        for row in range(extent):
            inverse[pl.ds(start + row * extent, half), :] = low[row]
            if row >= half:
                inverse[pl.ds(start + row * extent + half, half), :] = high[row]
            carry[pl.ds(start + row * extent, half), :] = beyond[row][0]
            carry[pl.ds(start + row * extent + half, half), :] = beyond[row][1]
            if row < half:
                schur[pl.ds(ahead + row * extent, half), :] = next_low[row]
            schur[pl.ds(ahead + row * extent + half, half), :] = next_high[row]
        return 0

    lax.fori_loop(0, middle - 1, advance, 0)
    pl.semaphore_wait(barrier, 4)

    def send(origin, target, number, device):
        return pltpu.make_async_remote_copy(
            src_ref=origin,
            dst_ref=target,
            send_sem=send_sems.at[number],
            recv_sem=recv_sems.at[number],
            device_id=device,
            device_id_type=MESH,
        )

    to_right = send(previous, from_left, 0, right)
    to_left = send(previous, from_right, 1, left)
    to_mirror = send(bottom, facing, 2, mirror)
    to_right.start()
    to_left.start()
    to_mirror.start()

    fetches[4].wait()
    fetches[5].wait()
    lax.fori_loop(middle - 1, depth, advance, 0)
    done = depth * extent * extent
    upper = half * extent
    block_out[0:upper, :] = schur[done : done + upper, :]
    for row in range(half):
        here = done + (half + row) * extent + half
        block_out[upper + row * half : upper + (row + 1) * half, :] = schur[here : here + half, :]
    to_across = send(block_out, block_in, 3, across)
    to_across.start()

    for fetch in late:
        fetch.wait()
    to_right.wait()
    to_left.wait()
    to_mirror.wait()
    own = previous[...]
    has_left = jnp.where(plane > 0, 1.0, 0.0).astype(jnp.float32)
    has_right = jnp.where(plane < planes - 1, 1.0, 0.0).astype(jnp.float32)
    span = lengths.shape[1]
    offline = (
        coupling[0] * (from_left[...] * has_left)
        + coupling[1] * (from_right[...] * has_right)
        + coupling[2] * pltpu.roll(own, 1, 1)
        + coupling[3] * pltpu.roll(own, span - 1, 1)
    )
    rows = extent * depth
    levels = lax.rem(lax.broadcasted_iota(jnp.int32, (rows, span), 0), depth) + base
    active = jnp.where(levels < lengths, 1.0, 0.0).astype(jnp.float32)
    source[...] = (residual[...] + offline) * active
    chosen = jnp.where(
        lax.broadcasted_iota(jnp.int32, (span, span), 0) == partner_map[...], 1.0, 0.0
    ).astype(jnp.float32)
    partner = jnp.dot(
        facing[...], chosen, precision=lax.Precision.HIGHEST, preferred_element_type=jnp.float32
    )
    first_rows = first.reshape(extent * extent * middle, span)
    wake = total(
        [
            first_rows[pl.ds(inner * middle, extent, stride=extent * middle), :]
            * spread(partner, inner, extent)
            for inner in range(extent)
        ]
    )
    weight = flag[...].astype(jnp.float32) * jnp.where(wall == 0, 1.0, 0.0).astype(jnp.float32)
    bottom_rows = pl.ds(0, extent, stride=depth)
    source[bottom_rows, :] = source[bottom_rows, :] - wake * weight * mask_at(base)

    def source_at(step):
        return source[pl.ds(level_at(step), extent, stride=depth), :]

    def halves_of(vector):
        return vector[:half], vector[half:]

    def spreads_of(vector):
        return [spread(vector[row // half], row % half, half) for row in range(extent)]

    def by_rows(spreads, store, start):
        return [
            total(
                [
                    spreads[row] * store[pl.ds(start + row * extent + part * half, half), :]
                    for row in range(extent)
                ]
            )
            for part in range(2)
        ]

    def by_columns(spreads, store, start):
        return [
            total(
                [
                    spreads[column]
                    * store[
                        pl.ds(start + part * half * extent + column, half, stride=extent), :
                    ]
                    for column in range(extent)
                ]
            )
            for part in range(2)
        ]

    def lower_rows(rows_low, rows_high, spreads):
        return [
            total([spreads[row] * rows_low(row) for row in range(extent)]),
            total([spreads[row] * rows_high(row) for row in range(half, extent)]),
        ]

    def forward(step, vector):
        start = pl.multiple_of(step * (extent * extent), extent * extent)
        at = pl.multiple_of(step * extent, extent)
        reduced[pl.ds(at, half), :] = vector[0]
        reduced[pl.ds(at + half, half), :] = vector[1]
        spreads = spreads_of(vector)
        lifted = [
            total(
                [
                    spreads[column]
                    * inverse[pl.ds(start + part * half * extent + column, half, stride=extent), :]
                    for column in range(half * (part + 1))
                ]
            )
            for part in range(2)
        ]
        for part in range(2):
            here = pl.ds(at + part * half, half)
            fixed[here, :] = lifted[part] * scale[here, :]
        change = by_rows(spreads_of(lifted), carry, start)
        vector_out[0:half, :] = change[0]
        vector_out[half:extent, :] = change[1]
        following = halves_of(source_at(jnp.minimum(step + 1, depth - 1)))
        return tuple(given - less for given, less in zip(following, change))

    lax.fori_loop(0, depth, forward, halves_of(source_at(0)))
    vector_across = send(vector_out, vector_in, 4, across)
    vector_across.start()

    to_across.wait()
    last = (depth - 1) * extent * extent
    low, high = [], []
    for row in range(extent):
        here = last + row * extent
        if row < half:
            low.append(schur[here : here + half, :] + block_in[row * extent : row * extent + half, :])
            high.append(
                schur[here + half : here + extent, :]
                + block_in[row * extent + half : (row + 1) * extent, :]
            )
        else:
            low.append(None)
            at = upper + (row - half) * half
            high.append(schur[here + half : here + extent, :] + block_in[at : at + half, :])
    scales = factor(low, high, None, None)
    for row in range(extent):
        inverse[last + row * extent : last + row * extent + half, :] = low[row]
        if row >= half:
            inverse[last + row * extent + half : last + (row + 1) * extent, :] = high[row]
    vector_across.wait()
    spreads = spreads_of(
        halves_of(reduced[(depth - 1) * extent : depth * extent, :] - vector_in[...])
    )
    lifted = [
        total(
            [
                spreads[column]
                * inverse[pl.ds(last + part * half * extent + column, half, stride=extent), :]
                for column in range(half * (part + 1))
            ]
        )
        * scales[part]
        for part in range(2)
    ]

    def lowered(vector, start):
        return lower_rows(
            lambda row: inverse[pl.ds(start + row * extent, half), :],
            lambda row: inverse[pl.ds(start + row * extent + half, half), :],
            spreads_of(vector),
        )

    def put(step, value):
        out[pl.ds(level_at(step), half, stride=depth), :] = value[0]
        out[pl.ds(level_at(step) + half * depth, half, stride=depth), :] = value[1]

    value = lowered(lifted, last)
    put(depth - 1, value)

    def backward(count, value):
        step = depth - 2 - count
        start = pl.multiple_of(step * (extent * extent), extent * extent)
        at = pl.multiple_of(step * extent, extent)
        change = by_columns(spreads_of(value), carry, start)
        given = [fixed[pl.ds(at + part * half, half), :] - change[part] for part in range(2)]
        value = lowered(given, start)
        put(step, value)
        return tuple(value)

    lax.fori_loop(0, depth - 1, backward, tuple(value))


def per_device(
    jacobian, residual, previous_update, offline_coupling, wake_partner, line_length, bottom_flag
):
    extent, depth, span = jacobian.shape[1], jacobian.shape[3], jacobian.shape[5]
    block = extent * extent
    whole = pl.BlockSpec(memory_space=pltpu.VMEM)
    f32 = jnp.float32

    def room(rows):
        return pltpu.VMEM((rows, span), f32)

    result = pl.pallas_call(
        functools.partial(kernel, extent, depth),
        out_shape=jax.ShapeDtypeStruct((extent * depth, span), f32),
        in_specs=[pl.BlockSpec(memory_space=pl.ANY)] * 7,
        out_specs=whole,
        scratch_shapes=[
            room(extent * depth),
            room(extent * depth),
            pltpu.VMEM((4, extent * depth, span), f32),
            pltpu.VMEM((1, span), jnp.int32),
            pltpu.VMEM((1, span), jnp.int32),
            pltpu.VMEM((1, span), jnp.int32),
            pltpu.VMEM((block, depth, span), f32),
            pltpu.VMEM((block, depth, span), f32),
            pltpu.VMEM((block, depth // 2, span), f32),
            room(block * (depth + 1)),
            room(block * depth),
            room(block * depth),
            room(extent * depth),
            room(extent * depth),
            room(extent * depth),
            room(extent * depth),
            room(extent),
            room(extent),
            room(extent * depth),
            room(extent * depth),
            room(block * 3 // 4),
            room(block * 3 // 4),
            room(extent),
            room(extent),
            pltpu.SemaphoreType.DMA((11,)),
            pltpu.SemaphoreType.DMA((5,)),
            pltpu.SemaphoreType.DMA((5,)),
        ],
        compiler_params=pltpu.CompilerParams(
            collective_id=0, has_side_effects=True, vmem_limit_bytes=63 * 1024 * 1024
        ),
    )(
        jacobian.reshape(3, block, depth, span),
        residual.reshape(extent * depth, span),
        previous_update.reshape(extent * depth, span),
        offline_coupling.reshape(4, extent * depth, span),
        wake_partner,
        line_length,
        bottom_flag,
    )
    return result.reshape(extent, depth, 1, span)


def solution(mesh):
    return jax.shard_map(
        per_device,
        mesh=mesh,
        in_specs=(
            P(None, None, None, "wall", "plane", None),
            P(None, "wall", "plane", None),
            P(None, "wall", "plane", None),
            P(None, None, "wall", "plane", None),
            P("plane", None),
            P("plane", None),
            P("plane", None),
        ),
        out_specs=P(None, "wall", "plane", None),
        check_vma=False,
    )
```

```python
import functools

import jax
import jax.numpy as jnp
from jax import lax
from jax.experimental import pallas as pl
from jax.experimental.pallas import tpu as pltpu
from jax.sharding import PartitionSpec as P

MESH = pl.DeviceIdType.MESH


def spread(row, index, rows):
    return jnp.broadcast_to(row[index : index + 1, :], (rows, row.shape[1]))


def factor(low, high, right, following):
    extent = len(high)
    half = high[0].shape[0]
    group = 4
    place = lax.broadcasted_iota(jnp.int32, high[0].shape, 0)
    scales = [jnp.zeros_like(high[0]), jnp.zeros_like(high[0])]

    def entry(row, column):
        return spread(low[row] if column < half else high[row], column % half, half)

    inverse = 1.0 / entry(0, 0)
    finished = []
    for pivot in range(extent):
        in_low = pivot < half
        at = pivot % half
        here = place == at
        pivot_low, pivot_high = low[pivot], high[pivot]
        if pivot + 1 < extent:
            beside = entry(pivot, pivot + 1)
            next_inverse = 1.0 / (entry(pivot + 1, pivot + 1) - beside * (beside * inverse))
        scales[pivot // half] = jnp.where(here, inverse, scales[pivot // half])
        scaled_low, scaled_high = pivot_low * inverse, pivot_high * inverse
        if in_low:
            scaled_low = jnp.where(here, inverse, scaled_low)
            known_low = jnp.where(place <= at, scaled_low, 0.0)
            low[pivot] = jnp.where(place < at, pivot_low, jnp.where(here, 1.0, 0.0))
            high[pivot] = None
        else:
            scaled_high = jnp.where(here, inverse, scaled_high)
            high[pivot] = jnp.where(place < at, pivot_high, jnp.where(here, 1.0, 0.0))
        if right is not None:
            scaled_right = tuple(part * inverse for part in right[pivot])
            finished.append((right[pivot], scaled_right))
            right[pivot] = scaled_right
        for row in range(pivot + 1, extent):
            by = spread(pivot_low if row < half else pivot_high, row % half, half)
            if row < half:
                low[row] = jnp.where(here, 0.0, low[row]) - by * scaled_low
                high[row] = high[row] - by * scaled_high
            elif in_low:
                low[row] = -(by * known_low) if pivot == 0 else low[row] - by * known_low
                high[row] = high[row] - by * scaled_high
            else:
                low[row] = low[row] - by * scaled_low
                high[row] = jnp.where(here, 0.0, high[row]) - by * scaled_high
            if right is not None:
                right[row] = tuple(
                    part - by * scaled for part, scaled in zip(right[row], scaled_right)
                )
        if len(finished) == group:
            next_low, next_high = following
            for row in range(extent):
                bys = [spread(plain[row // half], row % half, half) for plain, _ in finished]
                if row < half:
                    next_low[row] = next_low[row] - total(
                        [by * scaled[0] for by, (_, scaled) in zip(bys, finished)]
                    )
                next_high[row] = next_high[row] - total(
                    [by * scaled[1] for by, (_, scaled) in zip(bys, finished)]
                )
            finished = []
        inverse = next_inverse
    return scales


def total(terms):
    while len(terms) > 1:
        terms = [
            terms[at] + terms[at + 1] if at + 1 < len(terms) else terms[at]
            for at in range(0, len(terms), 2)
        ]
    return terms[0]


def kernel(
    extent,
    depth,
    jacobian,
    residual_far,
    previous_far,
    coupling_far,
    partner_far,
    length_far,
    flag_far,
    out,
    residual,
    previous,
    coupling,
    partner_map,
    length,
    flag,
    near_store,
    centre_store,
    first,
    schur,
    inverse,
    carry,
    source,
    reduced,
    fixed,
    scale,
    bottom,
    facing,
    from_left,
    from_right,
    block_out,
    block_in,
    vector_out,
    vector_in,
    copy_sems,
    send_sems,
    recv_sems,
):
    wall = lax.axis_index("wall")
    plane = lax.axis_index("plane")
    planes = lax.axis_size("plane")
    half = extent // 2
    has_left, has_right = plane > 0, plane < planes - 1
    right = {"wall": wall, "plane": plane + 1}
    left = {"wall": wall, "plane": plane - 1}
    mirror = {"wall": wall, "plane": lax.rem(plane + planes // 2, planes)}
    across = {"wall": 1 - wall, "plane": plane}

    near = near_store.reshape(extent * extent * depth, near_store.shape[2])
    centre = centre_store.reshape(extent * extent * depth, near_store.shape[2])
    middle = depth // 2
    halves = [pl.multiple_of(wall * middle, middle), pl.multiple_of((1 - wall) * middle, middle)]
    near_at = 2 - 2 * wall
    fetches = [
        pltpu.make_async_copy(previous_far, previous, copy_sems.at[0]),
        pltpu.make_async_copy(length_far, length, copy_sems.at[1]),
    ]
    for at, part in enumerate(halves):
        levels_here = pl.ds(part, middle)
        fetches.append(
            pltpu.make_async_copy(
                jacobian.at[1, :, levels_here], centre_store.at[:, levels_here], copy_sems.at[2 + 2 * at]
            )
        )
        fetches.append(
            pltpu.make_async_copy(
                jacobian.at[near_at, :, levels_here],
                near_store.at[:, levels_here],
                copy_sems.at[3 + 2 * at],
            )
        )
    first_fetch = pltpu.make_async_copy(
        jacobian.at[0, :, pl.ds(0, middle)], first, copy_sems.at[6]
    )
    late = [
        pltpu.make_async_copy(residual_far, residual, copy_sems.at[7]),
        pltpu.make_async_copy(coupling_far, coupling, copy_sems.at[8]),
        pltpu.make_async_copy(partner_far, partner_map, copy_sems.at[9]),
        pltpu.make_async_copy(flag_far, flag, copy_sems.at[10]),
    ]
    fetches[1].start()
    fetches[2].start()
    fetches[3].start()
    fetches[0].start()

    barrier = pltpu.get_barrier_semaphore()

    def greet(device):
        pl.semaphore_signal(barrier, inc=1, device_id=device, device_id_type=MESH)

    greet(across)
    pl.when(wall == 0)(lambda: greet(mirror))
    pl.when(has_left)(lambda: greet(left))
    pl.when(has_right)(lambda: greet(right))
    greetings = (
        1 + (wall == 0).astype(jnp.int32) + has_left.astype(jnp.int32) + has_right.astype(jnp.int32)
    )

    @pl.when(jnp.logical_not(has_left))
    def _():
        from_left[...] = jnp.zeros_like(from_left)

    @pl.when(jnp.logical_not(has_right))
    def _():
        from_right[...] = jnp.zeros_like(from_right)

    def send(origin, target, number, device):
        return pltpu.make_async_remote_copy(
            src_ref=origin,
            dst_ref=target,
            send_sem=send_sems.at[number],
            recv_sem=recv_sems.at[number],
            device_id=device,
            device_id_type=MESH,
        )

    to_right = send(previous, from_left, 0, right)
    to_left = send(previous, from_right, 1, left)
    to_mirror = send(bottom, facing, 2, mirror)
    fetches[1].wait()

    lengths = length[...]
    base = wall * depth

    def level_at(step):
        return step + wall * (depth - 1 - 2 * step)

    def mask_at(level):
        return jnp.where(level < lengths, 1.0, 0.0).astype(jnp.float32)

    place = lax.broadcasted_iota(jnp.int32, (extent, lengths.shape[1]), 0)

    def diagonal(step, row):
        level = level_at(step)
        mask = mask_at(level + base)
        block = centre[pl.ds(row * extent * depth + level, extent, stride=depth), :]
        return block * mask + jnp.where(place == row, 1.0 - mask, 0.0)

    fetches[2].wait()
    for row in range(extent):
        schur[pl.ds(row * extent, extent), :] = diagonal(0, row)
    fetches[3].wait()
    fetches[4].start()
    fetches[5].start()
    pl.when(wall == 0)(first_fetch.start)
    for fetch in late:
        fetch.start()
    fetches[0].wait()
    bottom[...] = previous[pl.ds(0, extent, stride=depth), :]

    def advance(step, _):
        @pl.when(step == 3)
        def _():
            pl.semaphore_wait(barrier, greetings)
            pl.when(has_right)(to_right.start)
            pl.when(has_left)(to_left.start)
            pl.when(wall == 0)(to_mirror.start)

        @pl.when(step == middle - 1)
        def _():
            fetches[4].wait()
            fetches[5].wait()

        level = level_at(step)
        start = pl.multiple_of(step * (extent * extent), extent * extent)
        mask = mask_at(level + base + 1 - wall)
        low, high, beyond = [], [], []
        next_low, next_high = [], []
        following = jnp.minimum(step + 1, depth - 1)
        kept = jnp.where(step < depth - 1, 1.0, 0.0).astype(jnp.float32)
        for row in range(extent):
            low.append(schur[pl.ds(start + row * extent, half), :] if row < half else None)
            high.append(schur[pl.ds(start + row * extent + half, half), :])
            block = near[pl.ds(row * extent * depth + level, extent, stride=depth), :] * mask
            beyond.append((block[:half], block[half:]))
            block = diagonal(following, row) * kept
            next_low.append(block[:half])
            next_high.append(block[half:])
        scales = factor(low, high, beyond, (next_low, next_high))
        ahead = pl.multiple_of((step + 1) * (extent * extent), extent * extent)
        scale_at = pl.multiple_of(step * extent, extent)
        scale[pl.ds(scale_at, half), :] = scales[0]
        scale[pl.ds(scale_at + half, half), :] = scales[1]
        for row in range(extent):
            inverse[pl.ds(start + row * extent, half), :] = low[row]
            if row >= half:
                inverse[pl.ds(start + row * extent + half, half), :] = high[row]
            carry[pl.ds(start + row * extent, half), :] = beyond[row][0]
            carry[pl.ds(start + row * extent + half, half), :] = beyond[row][1]
            if row < half:
                schur[pl.ds(ahead + row * extent, half), :] = next_low[row]
            schur[pl.ds(ahead + row * extent + half, half), :] = next_high[row]
        return 0

    lax.fori_loop(0, depth, advance, 0)
    done = depth * extent * extent
    upper = half * extent
    block_out[0:upper, :] = schur[done : done + upper, :]
    for row in range(half):
        here = done + (half + row) * extent + half
        block_out[upper + row * half : upper + (row + 1) * half, :] = schur[here : here + half, :]
    to_across = send(block_out, block_in, 3, across)
    to_across.start()

    for fetch in late:
        fetch.wait()

    @pl.when(has_right)
    def _():
        to_right.wait_send()
        to_left.wait_recv()

    @pl.when(has_left)
    def _():
        to_left.wait_send()
        to_right.wait_recv()

    own = previous[...]
    span = lengths.shape[1]
    offline = (
        coupling[0] * from_left[...]
        + coupling[1] * from_right[...]
        + coupling[2] * pltpu.roll(own, 1, 1)
        + coupling[3] * pltpu.roll(own, span - 1, 1)
    )
    rows = extent * depth
    levels = lax.rem(lax.broadcasted_iota(jnp.int32, (rows, span), 0), depth) + base
    active = jnp.where(levels < lengths, 1.0, 0.0).astype(jnp.float32)
    source[...] = (residual[...] + offline) * active
    @pl.when(wall == 0)
    def _():
        first_fetch.wait()
        to_mirror.wait()
        chosen = jnp.where(
            lax.broadcasted_iota(jnp.int32, (span, span), 0) == partner_map[...], 1.0, 0.0
        ).astype(jnp.float32)
        partner = jnp.dot(
            facing[...], chosen, precision=lax.Precision.HIGHEST, preferred_element_type=jnp.float32
        )
        first_rows = first.reshape(extent * extent * middle, span)
        wake = total(
            [
                first_rows[pl.ds(inner * middle, extent, stride=extent * middle), :]
                * spread(partner, inner, extent)
                for inner in range(extent)
            ]
        )
        weight = flag[...].astype(jnp.float32)
        bottom_rows = pl.ds(0, extent, stride=depth)
        source[bottom_rows, :] = source[bottom_rows, :] - wake * weight * mask_at(base)

    def source_at(step):
        return source[pl.ds(level_at(step), extent, stride=depth), :]

    def halves_of(vector):
        return vector[:half], vector[half:]

    def spreads_of(vector):
        return [spread(vector[row // half], row % half, half) for row in range(extent)]

    def by_rows(spreads, store, start):
        return [
            total(
                [
                    spreads[row] * store[pl.ds(start + row * extent + part * half, half), :]
                    for row in range(extent)
                ]
            )
            for part in range(2)
        ]

    def by_columns(spreads, store, start):
        return [
            total(
                [
                    spreads[column]
                    * store[
                        pl.ds(start + part * half * extent + column, half, stride=extent), :
                    ]
                    for column in range(extent)
                ]
            )
            for part in range(2)
        ]

    def lower_rows(rows_low, rows_high, spreads):
        return [
            total([spreads[row] * rows_low(row) for row in range(extent)]),
            total([spreads[row] * rows_high(row) for row in range(half, extent)]),
        ]

    def forward(step, vector):
        start = pl.multiple_of(step * (extent * extent), extent * extent)
        at = pl.multiple_of(step * extent, extent)
        reduced[pl.ds(at, half), :] = vector[0]
        reduced[pl.ds(at + half, half), :] = vector[1]
        spreads = spreads_of(vector)
        lifted = [
            total(
                [
                    spreads[column]
                    * inverse[pl.ds(start + part * half * extent + column, half, stride=extent), :]
                    for column in range(half * (part + 1))
                ]
            )
            for part in range(2)
        ]
        for part in range(2):
            here = pl.ds(at + part * half, half)
            fixed[here, :] = lifted[part] * scale[here, :]
        change = by_rows(spreads_of(lifted), carry, start)
        vector_out[0:half, :] = change[0]
        vector_out[half:extent, :] = change[1]
        following = halves_of(source_at(jnp.minimum(step + 1, depth - 1)))
        return tuple(given - less for given, less in zip(following, change))

    lax.fori_loop(0, depth, forward, halves_of(source_at(0)))
    vector_across = send(vector_out, vector_in, 4, across)
    vector_across.start()

    to_across.wait()
    last = (depth - 1) * extent * extent
    low, high = [], []
    for row in range(extent):
        here = last + row * extent
        if row < half:
            low.append(schur[here : here + half, :] + block_in[row * extent : row * extent + half, :])
            high.append(
                schur[here + half : here + extent, :]
                + block_in[row * extent + half : (row + 1) * extent, :]
            )
        else:
            low.append(None)
            at = upper + (row - half) * half
            high.append(schur[here + half : here + extent, :] + block_in[at : at + half, :])
    scales = factor(low, high, None, None)
    for row in range(extent):
        inverse[last + row * extent : last + row * extent + half, :] = low[row]
        if row >= half:
            inverse[last + row * extent + half : last + (row + 1) * extent, :] = high[row]
    vector_across.wait()
    spreads = spreads_of(
        halves_of(reduced[(depth - 1) * extent : depth * extent, :] - vector_in[...])
    )
    lifted = [
        total(
            [
                spreads[column]
                * inverse[pl.ds(last + part * half * extent + column, half, stride=extent), :]
                for column in range(half * (part + 1))
            ]
        )
        * scales[part]
        for part in range(2)
    ]

    def lowered(vector, start):
        return lower_rows(
            lambda row: inverse[pl.ds(start + row * extent, half), :],
            lambda row: inverse[pl.ds(start + row * extent + half, half), :],
            spreads_of(vector),
        )

    def put(step, value):
        out[pl.ds(level_at(step), half, stride=depth), :] = value[0]
        out[pl.ds(level_at(step) + half * depth, half, stride=depth), :] = value[1]

    value = lowered(lifted, last)
    put(depth - 1, value)

    def backward(count, value):
        step = depth - 2 - count
        start = pl.multiple_of(step * (extent * extent), extent * extent)
        at = pl.multiple_of(step * extent, extent)
        change = by_columns(spreads_of(value), carry, start)
        given = [fixed[pl.ds(at + part * half, half), :] - change[part] for part in range(2)]
        value = lowered(given, start)
        put(step, value)
        return tuple(value)

    lax.fori_loop(0, depth - 1, backward, tuple(value))


def per_device(
    jacobian, residual, previous_update, offline_coupling, wake_partner, line_length, bottom_flag
):
    extent, depth, span = jacobian.shape[1], jacobian.shape[3], jacobian.shape[5]
    block = extent * extent
    whole = pl.BlockSpec(memory_space=pltpu.VMEM)
    f32 = jnp.float32

    def room(rows):
        return pltpu.VMEM((rows, span), f32)

    result = pl.pallas_call(
        functools.partial(kernel, extent, depth),
        out_shape=pltpu.VMEM((extent * depth, span), f32),
        in_specs=[pl.BlockSpec(memory_space=pl.ANY)] * 7,
        out_specs=whole,
        scratch_shapes=[
            room(extent * depth),
            room(extent * depth),
            pltpu.VMEM((4, extent * depth, span), f32),
            pltpu.VMEM((1, span), jnp.int32),
            pltpu.VMEM((1, span), jnp.int32),
            pltpu.VMEM((1, span), jnp.int32),
            pltpu.VMEM((block, depth, span), f32),
            pltpu.VMEM((block, depth, span), f32),
            pltpu.VMEM((block, depth // 2, span), f32),
            room(block * (depth + 1)),
            room(block * depth),
            room(block * depth),
            room(extent * depth),
            room(extent * depth),
            room(extent * depth),
            room(extent * depth),
            room(extent),
            room(extent),
            room(extent * depth),
            room(extent * depth),
            room(block * 3 // 4),
            room(block * 3 // 4),
            room(extent),
            room(extent),
            pltpu.SemaphoreType.DMA((11,)),
            pltpu.SemaphoreType.DMA((5,)),
            pltpu.SemaphoreType.DMA((5,)),
        ],
        compiler_params=pltpu.CompilerParams(
            collective_id=0, has_side_effects=True, vmem_limit_bytes=63 * 1024 * 1024
        ),
    )(
        jacobian.reshape(3, block, depth, span),
        residual.reshape(extent * depth, span),
        previous_update.reshape(extent * depth, span),
        offline_coupling.reshape(4, extent * depth, span),
        wake_partner,
        line_length,
        bottom_flag,
    )
    return result.reshape(extent, depth, 1, span)


def solution(mesh):
    return jax.shard_map(
        per_device,
        mesh=mesh,
        in_specs=(
            P(None, None, None, "wall", "plane", None),
            P(None, "wall", "plane", None),
            P(None, "wall", "plane", None),
            P(None, None, "wall", "plane", None),
            P("plane", None),
            P("plane", None),
            P("plane", None),
        ),
        out_specs=P(None, "wall", "plane", None),
        check_vma=False,
    )
```

```python
import functools

import jax
import jax.numpy as jnp
from jax import lax
from jax.experimental import pallas as pl
from jax.experimental.pallas import tpu as pltpu
from jax.sharding import PartitionSpec as P

MESH = pl.DeviceIdType.MESH


def spread(row, index, rows):
    return jnp.broadcast_to(row[index : index + 1, :], (rows, row.shape[1]))


def factor(low, high, right, following):
    extent = len(high)
    half = high[0].shape[0]
    group = 4
    place = lax.broadcasted_iota(jnp.int32, high[0].shape, 0)
    scales = [jnp.zeros_like(high[0]), jnp.zeros_like(high[0])]

    def entry(row, column):
        return spread(low[row] if column < half else high[row], column % half, half)

    inverse = 1.0 / entry(0, 0)
    finished = []
    for pivot in range(extent):
        in_low = pivot < half
        at = pivot % half
        here = place == at
        pivot_low, pivot_high = low[pivot], high[pivot]
        if pivot + 1 < extent:
            beside = entry(pivot, pivot + 1)
            next_inverse = 1.0 / (entry(pivot + 1, pivot + 1) - beside * (beside * inverse))
        scales[pivot // half] = jnp.where(here, inverse, scales[pivot // half])
        scaled_low, scaled_high = pivot_low * inverse, pivot_high * inverse
        if in_low:
            scaled_low = jnp.where(here, inverse, scaled_low)
            known_low = jnp.where(place <= at, scaled_low, 0.0)
            low[pivot] = jnp.where(place < at, pivot_low, jnp.where(here, 1.0, 0.0))
            high[pivot] = None
        else:
            scaled_high = jnp.where(here, inverse, scaled_high)
            high[pivot] = jnp.where(place < at, pivot_high, jnp.where(here, 1.0, 0.0))
        if right is not None:
            scaled_right = tuple(part * inverse for part in right[pivot])
            finished.append((right[pivot], scaled_right))
            right[pivot] = scaled_right
        for row in range(pivot + 1, extent):
            by = spread(pivot_low if row < half else pivot_high, row % half, half)
            if row < half:
                low[row] = jnp.where(here, 0.0, low[row]) - by * scaled_low
                high[row] = high[row] - by * scaled_high
            elif in_low:
                low[row] = -(by * known_low) if pivot == 0 else low[row] - by * known_low
                high[row] = high[row] - by * scaled_high
            else:
                low[row] = low[row] - by * scaled_low
                high[row] = jnp.where(here, 0.0, high[row]) - by * scaled_high
            if right is not None:
                right[row] = tuple(
                    part - by * scaled for part, scaled in zip(right[row], scaled_right)
                )
        if len(finished) == group:
            next_low, next_high = following
            for row in range(extent):
                bys = [spread(plain[row // half], row % half, half) for plain, _ in finished]
                if row < half:
                    next_low[row] = next_low[row] - total(
                        [by * scaled[0] for by, (_, scaled) in zip(bys, finished)]
                    )
                next_high[row] = next_high[row] - total(
                    [by * scaled[1] for by, (_, scaled) in zip(bys, finished)]
                )
            finished = []
        inverse = next_inverse
    return scales


def total(terms):
    while len(terms) > 1:
        terms = [
            terms[at] + terms[at + 1] if at + 1 < len(terms) else terms[at]
            for at in range(0, len(terms), 2)
        ]
    return terms[0]


def kernel(
    extent,
    depth,
    jacobian,
    residual_far,
    previous_far,
    coupling_far,
    partner_far,
    length_far,
    flag_far,
    out,
    residual,
    previous,
    coupling,
    partner_map,
    length,
    flag,
    near_store,
    centre_store,
    first,
    schur,
    inverse,
    carry,
    source,
    reduced,
    fixed,
    scale,
    bottom,
    facing,
    from_left,
    from_right,
    block_out,
    block_in,
    vector_out,
    vector_in,
    copy_sems,
    send_sems,
    recv_sems,
):
    wall = lax.axis_index("wall")
    plane = lax.axis_index("plane")
    planes = lax.axis_size("plane")
    half = extent // 2
    has_left, has_right = plane > 0, plane < planes - 1
    right = {"wall": wall, "plane": plane + 1}
    left = {"wall": wall, "plane": plane - 1}
    mirror = {"wall": wall, "plane": lax.rem(plane + planes // 2, planes)}
    across = {"wall": 1 - wall, "plane": plane}

    near = near_store.reshape(extent * extent * depth, near_store.shape[2])
    centre = centre_store.reshape(extent * extent * depth, near_store.shape[2])
    middle = depth // 2
    halves = [pl.multiple_of(wall * middle, middle), pl.multiple_of((1 - wall) * middle, middle)]
    near_at = 2 - 2 * wall
    fetches = [
        pltpu.make_async_copy(previous_far, previous, copy_sems.at[0]),
        pltpu.make_async_copy(length_far, length, copy_sems.at[1]),
    ]
    for at, part in enumerate(halves):
        levels_here = pl.ds(part, middle)
        fetches.append(
            pltpu.make_async_copy(
                jacobian.at[1, :, levels_here], centre_store.at[:, levels_here], copy_sems.at[2 + 2 * at]
            )
        )
        fetches.append(
            pltpu.make_async_copy(
                jacobian.at[near_at, :, levels_here],
                near_store.at[:, levels_here],
                copy_sems.at[3 + 2 * at],
            )
        )
    first_fetch = pltpu.make_async_copy(
        jacobian.at[0, :, pl.ds(0, middle)], first, copy_sems.at[6]
    )
    late = [
        pltpu.make_async_copy(residual_far, residual, copy_sems.at[7]),
        pltpu.make_async_copy(coupling_far, coupling, copy_sems.at[8]),
        pltpu.make_async_copy(partner_far, partner_map, copy_sems.at[9]),
        pltpu.make_async_copy(flag_far, flag, copy_sems.at[10]),
    ]
    fetches[1].start()
    fetches[2].start()
    fetches[3].start()
    fetches[0].start()

    barrier = pltpu.get_barrier_semaphore()

    def greet(device):
        pl.semaphore_signal(barrier, inc=1, device_id=device, device_id_type=MESH)

    greet(across)
    pl.when(wall == 0)(lambda: greet(mirror))
    pl.when(has_left)(lambda: greet(left))
    pl.when(has_right)(lambda: greet(right))
    greetings = (
        1 + (wall == 0).astype(jnp.int32) + has_left.astype(jnp.int32) + has_right.astype(jnp.int32)
    )

    @pl.when(jnp.logical_not(has_left))
    def _():
        from_left[...] = jnp.zeros_like(from_left)

    @pl.when(jnp.logical_not(has_right))
    def _():
        from_right[...] = jnp.zeros_like(from_right)

    def send(origin, target, number, device):
        return pltpu.make_async_remote_copy(
            src_ref=origin,
            dst_ref=target,
            send_sem=send_sems.at[number],
            recv_sem=recv_sems.at[number],
            device_id=device,
            device_id_type=MESH,
        )

    to_right = send(previous, from_left, 0, right)
    to_left = send(previous, from_right, 1, left)
    to_mirror = send(bottom, facing, 2, mirror)
    fetches[1].wait()

    lengths = length[...]
    base = wall * depth

    def level_at(step):
        return step + wall * (depth - 1 - 2 * step)

    def mask_at(level):
        return jnp.where(level < lengths, 1.0, 0.0).astype(jnp.float32)

    place = lax.broadcasted_iota(jnp.int32, (extent, lengths.shape[1]), 0)

    def diagonal(step, row):
        level = level_at(step)
        mask = mask_at(level + base)
        block = centre[pl.ds(row * extent * depth + level, extent, stride=depth), :]
        return block * mask + jnp.where(place == row, 1.0 - mask, 0.0)

    fetches[2].wait()
    started = [diagonal(0, row) for row in range(extent)]
    state = (
        tuple(block[:half] for block in started[:half]),
        tuple(block[half:] for block in started),
    )
    fetches[3].wait()
    fetches[4].start()
    fetches[5].start()
    pl.when(wall == 0)(first_fetch.start)
    for fetch in late:
        fetch.start()
    fetches[0].wait()
    bottom[...] = previous[pl.ds(0, extent, stride=depth), :]

    def keep_state(store, state):
        for row in range(half):
            store[row * half : (row + 1) * half, :] = state[0][row]
        for row in range(extent):
            here = (half + row) * half
            store[here : here + half, :] = state[1][row]

    def advance(step, state):
        @pl.when(step == 3)
        def _():
            pl.semaphore_wait(barrier, greetings)
            pl.when(has_right)(to_right.start)
            pl.when(has_left)(to_left.start)
            pl.when(wall == 0)(to_mirror.start)

        @pl.when(step == middle - 1)
        def _():
            fetches[4].wait()
            fetches[5].wait()

        level = level_at(step)
        start = pl.multiple_of(step * (extent * extent), extent * extent)
        mask = mask_at(level + base + 1 - wall)
        low, high = list(state[0]) + [None] * half, list(state[1])
        beyond, next_low, next_high = [], [], []
        keep_state(schur, state)
        following = jnp.minimum(step + 1, depth - 1)
        kept = jnp.where(step < depth - 1, 1.0, 0.0).astype(jnp.float32)
        for row in range(extent):
            block = near[pl.ds(row * extent * depth + level, extent, stride=depth), :] * mask
            beyond.append((block[:half], block[half:]))
            block = diagonal(following, row) * kept
            if row < half:
                next_low.append(block[:half])
            next_high.append(block[half:])
        scales = factor(low, high, beyond, (next_low, next_high))
        scale_at = pl.multiple_of(step * extent, extent)
        scale[pl.ds(scale_at, half), :] = scales[0]
        scale[pl.ds(scale_at + half, half), :] = scales[1]
        for row in range(extent):
            inverse[pl.ds(start + row * extent, half), :] = low[row]
            if row >= half:
                inverse[pl.ds(start + row * extent + half, half), :] = high[row]
            carry[pl.ds(start + row * extent, half), :] = beyond[row][0]
            carry[pl.ds(start + row * extent + half, half), :] = beyond[row][1]
        return tuple(next_low), tuple(next_high)

    keep_state(block_out, lax.fori_loop(0, depth, advance, state, unroll=2))
    to_across = send(block_out, block_in, 3, across)
    to_across.start()

    for fetch in late:
        fetch.wait()

    @pl.when(has_right)
    def _():
        to_right.wait_send()
        to_left.wait_recv()

    @pl.when(has_left)
    def _():
        to_left.wait_send()
        to_right.wait_recv()

    own = previous[...]
    span = lengths.shape[1]
    offline = (
        coupling[0] * from_left[...]
        + coupling[1] * from_right[...]
        + coupling[2] * pltpu.roll(own, 1, 1)
        + coupling[3] * pltpu.roll(own, span - 1, 1)
    )
    rows = extent * depth
    levels = lax.rem(lax.broadcasted_iota(jnp.int32, (rows, span), 0), depth) + base
    active = jnp.where(levels < lengths, 1.0, 0.0).astype(jnp.float32)
    source[...] = (residual[...] + offline) * active
    @pl.when(wall == 0)
    def _():
        first_fetch.wait()
        to_mirror.wait()
        chosen = jnp.where(
            lax.broadcasted_iota(jnp.int32, (span, span), 0) == partner_map[...], 1.0, 0.0
        ).astype(jnp.float32)
        partner = jnp.dot(
            facing[...], chosen, precision=lax.Precision.HIGHEST, preferred_element_type=jnp.float32
        )
        first_rows = first.reshape(extent * extent * middle, span)
        wake = total(
            [
                first_rows[pl.ds(inner * middle, extent, stride=extent * middle), :]
                * spread(partner, inner, extent)
                for inner in range(extent)
            ]
        )
        weight = flag[...].astype(jnp.float32)
        bottom_rows = pl.ds(0, extent, stride=depth)
        source[bottom_rows, :] = source[bottom_rows, :] - wake * weight * mask_at(base)

    def source_at(step):
        return source[pl.ds(level_at(step), extent, stride=depth), :]

    def halves_of(vector):
        return vector[:half], vector[half:]

    def spreads_of(vector):
        return [spread(vector[row // half], row % half, half) for row in range(extent)]

    def by_rows(spreads, store, start):
        return [
            total(
                [
                    spreads[row] * store[pl.ds(start + row * extent + part * half, half), :]
                    for row in range(extent)
                ]
            )
            for part in range(2)
        ]

    def by_columns(spreads, store, start):
        return [
            total(
                [
                    spreads[column]
                    * store[
                        pl.ds(start + part * half * extent + column, half, stride=extent), :
                    ]
                    for column in range(extent)
                ]
            )
            for part in range(2)
        ]

    def lower_rows(rows_low, rows_high, spreads):
        return [
            total([spreads[row] * rows_low(row) for row in range(extent)]),
            total([spreads[row] * rows_high(row) for row in range(half, extent)]),
        ]

    def forward(step, vector):
        start = pl.multiple_of(step * (extent * extent), extent * extent)
        at = pl.multiple_of(step * extent, extent)
        reduced[pl.ds(at, half), :] = vector[0]
        reduced[pl.ds(at + half, half), :] = vector[1]
        spreads = spreads_of(vector)
        lifted = [
            total(
                [
                    spreads[column]
                    * inverse[pl.ds(start + part * half * extent + column, half, stride=extent), :]
                    for column in range(half * (part + 1))
                ]
            )
            for part in range(2)
        ]
        for part in range(2):
            here = pl.ds(at + part * half, half)
            fixed[here, :] = lifted[part] * scale[here, :]
        change = by_rows(spreads_of(lifted), carry, start)
        vector_out[0:half, :] = change[0]
        vector_out[half:extent, :] = change[1]
        following = halves_of(source_at(jnp.minimum(step + 1, depth - 1)))
        return tuple(given - less for given, less in zip(following, change))

    lax.fori_loop(0, depth, forward, halves_of(source_at(0)))
    vector_across = send(vector_out, vector_in, 4, across)
    vector_across.start()

    to_across.wait()
    last = (depth - 1) * extent * extent
    met = schur[...] + block_in[...]
    low = [met[row * half : (row + 1) * half] for row in range(half)] + [None] * half
    high = [met[(half + row) * half : (half + row + 1) * half] for row in range(extent)]
    scales = factor(low, high, None, None)
    for row in range(extent):
        inverse[last + row * extent : last + row * extent + half, :] = low[row]
        if row >= half:
            inverse[last + row * extent + half : last + (row + 1) * extent, :] = high[row]
    vector_across.wait()
    spreads = spreads_of(
        halves_of(reduced[(depth - 1) * extent : depth * extent, :] - vector_in[...])
    )
    lifted = [
        total(
            [
                spreads[column]
                * inverse[pl.ds(last + part * half * extent + column, half, stride=extent), :]
                for column in range(half * (part + 1))
            ]
        )
        * scales[part]
        for part in range(2)
    ]

    def lowered(vector, start):
        return lower_rows(
            lambda row: inverse[pl.ds(start + row * extent, half), :],
            lambda row: inverse[pl.ds(start + row * extent + half, half), :],
            spreads_of(vector),
        )

    def put(step, value):
        out[pl.ds(level_at(step), half, stride=depth), :] = value[0]
        out[pl.ds(level_at(step) + half * depth, half, stride=depth), :] = value[1]

    value = lowered(lifted, last)
    put(depth - 1, value)

    def backward(count, value):
        step = depth - 2 - count
        start = pl.multiple_of(step * (extent * extent), extent * extent)
        at = pl.multiple_of(step * extent, extent)
        change = by_columns(spreads_of(value), carry, start)
        given = [fixed[pl.ds(at + part * half, half), :] - change[part] for part in range(2)]
        value = lowered(given, start)
        put(step, value)
        return tuple(value)

    lax.fori_loop(0, depth - 1, backward, tuple(value))


def per_device(
    jacobian, residual, previous_update, offline_coupling, wake_partner, line_length, bottom_flag
):
    extent, depth, span = jacobian.shape[1], jacobian.shape[3], jacobian.shape[5]
    block = extent * extent
    whole = pl.BlockSpec(memory_space=pltpu.VMEM)
    f32 = jnp.float32

    def room(rows):
        return pltpu.VMEM((rows, span), f32)

    result = pl.pallas_call(
        functools.partial(kernel, extent, depth),
        out_shape=pltpu.VMEM((extent * depth, span), f32),
        in_specs=[pl.BlockSpec(memory_space=pl.ANY)] * 7,
        out_specs=whole,
        scratch_shapes=[
            room(extent * depth),
            room(extent * depth),
            pltpu.VMEM((4, extent * depth, span), f32),
            pltpu.VMEM((1, span), jnp.int32),
            pltpu.VMEM((1, span), jnp.int32),
            pltpu.VMEM((1, span), jnp.int32),
            pltpu.VMEM((block, depth, span), f32),
            pltpu.VMEM((block, depth, span), f32),
            pltpu.VMEM((block, depth // 2, span), f32),
            room(block * 3 // 4),
            room(block * depth),
            room(block * depth),
            room(extent * depth),
            room(extent * depth),
            room(extent * depth),
            room(extent * depth),
            room(extent),
            room(extent),
            room(extent * depth),
            room(extent * depth),
            room(block * 3 // 4),
            room(block * 3 // 4),
            room(extent),
            room(extent),
            pltpu.SemaphoreType.DMA((11,)),
            pltpu.SemaphoreType.DMA((5,)),
            pltpu.SemaphoreType.DMA((5,)),
        ],
        compiler_params=pltpu.CompilerParams(
            collective_id=0, has_side_effects=True, vmem_limit_bytes=63 * 1024 * 1024
        ),
    )(
        jacobian.reshape(3, block, depth, span),
        residual.reshape(extent * depth, span),
        previous_update.reshape(extent * depth, span),
        offline_coupling.reshape(4, extent * depth, span),
        wake_partner,
        line_length,
        bottom_flag,
    )
    return result.reshape(extent, depth, 1, span)


def solution(mesh):
    return jax.shard_map(
        per_device,
        mesh=mesh,
        in_specs=(
            P(None, None, None, "wall", "plane", None),
            P(None, "wall", "plane", None),
            P(None, "wall", "plane", None),
            P(None, None, "wall", "plane", None),
            P("plane", None),
            P("plane", None),
            P("plane", None),
        ),
        out_specs=P(None, "wall", "plane", None),
        check_vma=False,
    )
```

```python
import functools

import jax
import jax.numpy as jnp
from jax import lax
from jax.experimental import pallas as pl
from jax.experimental.pallas import tpu as pltpu
from jax.sharding import PartitionSpec as P

MESH = pl.DeviceIdType.MESH


def spread(row, index, rows):
    return jnp.broadcast_to(row[index : index + 1, :], (rows, row.shape[1]))


def factor(low, high, right, following):
    extent = len(high)
    half = high[0].shape[0]
    group = 4
    place = lax.broadcasted_iota(jnp.int32, high[0].shape, 0)
    scales = [jnp.zeros_like(high[0]), jnp.zeros_like(high[0])]

    def entry(row, column):
        return spread(low[row] if column < half else high[row], column % half, half)

    inverse = 1.0 / entry(0, 0)
    finished = []
    for pivot in range(extent):
        in_low = pivot < half
        at = pivot % half
        here = place == at
        pivot_low, pivot_high = low[pivot], high[pivot]
        if pivot + 1 < extent:
            beside = entry(pivot, pivot + 1)
            next_inverse = 1.0 / (entry(pivot + 1, pivot + 1) - beside * (beside * inverse))
        scales[pivot // half] = jnp.where(here, inverse, scales[pivot // half])
        scaled_low, scaled_high = pivot_low * inverse, pivot_high * inverse
        if in_low:
            scaled_low = jnp.where(here, inverse, scaled_low)
            known_low = jnp.where(place <= at, scaled_low, 0.0)
            low[pivot] = jnp.where(place < at, pivot_low, jnp.where(here, 1.0, 0.0))
            high[pivot] = None
        else:
            scaled_high = jnp.where(here, inverse, scaled_high)
            high[pivot] = jnp.where(place < at, pivot_high, jnp.where(here, 1.0, 0.0))
        if right is not None:
            scaled_right = tuple(part * inverse for part in right[pivot])
            finished.append((right[pivot], scaled_right))
            right[pivot] = scaled_right
        for row in range(pivot + 1, extent):
            by = spread(pivot_low if row < half else pivot_high, row % half, half)
            if row < half:
                low[row] = jnp.where(here, 0.0, low[row]) - by * scaled_low
                high[row] = high[row] - by * scaled_high
            elif in_low:
                low[row] = -(by * known_low) if pivot == 0 else low[row] - by * known_low
                high[row] = high[row] - by * scaled_high
            else:
                low[row] = low[row] - by * scaled_low
                high[row] = jnp.where(here, 0.0, high[row]) - by * scaled_high
            if right is not None:
                right[row] = tuple(
                    part - by * scaled for part, scaled in zip(right[row], scaled_right)
                )
        if len(finished) == group:
            next_low, next_high = following
            for row in range(extent):
                bys = [spread(plain[row // half], row % half, half) for plain, _ in finished]
                if row < half:
                    next_low[row] = next_low[row] - total(
                        [by * scaled[0] for by, (_, scaled) in zip(bys, finished)]
                    )
                next_high[row] = next_high[row] - total(
                    [by * scaled[1] for by, (_, scaled) in zip(bys, finished)]
                )
            finished = []
        inverse = next_inverse
    return scales


def total(terms):
    while len(terms) > 1:
        terms = [
            terms[at] + terms[at + 1] if at + 1 < len(terms) else terms[at]
            for at in range(0, len(terms), 2)
        ]
    return terms[0]


def kernel(
    extent,
    depth,
    jacobian,
    residual_far,
    previous_far,
    coupling_far,
    partner_far,
    length_far,
    flag_far,
    out,
    residual,
    previous,
    coupling,
    partner_map,
    length,
    flag,
    near_store,
    centre_store,
    first,
    schur,
    inverse,
    carry,
    source,
    reduced,
    fixed,
    scale,
    bottom,
    facing,
    from_left,
    from_right,
    block_out,
    block_in,
    vector_out,
    vector_in,
    copy_sems,
    send_sems,
    recv_sems,
):
    wall = lax.axis_index("wall")
    plane = lax.axis_index("plane")
    planes = lax.axis_size("plane")
    half = extent // 2
    has_left, has_right = plane > 0, plane < planes - 1
    right = {"wall": wall, "plane": plane + 1}
    left = {"wall": wall, "plane": plane - 1}
    mirror = {"wall": wall, "plane": lax.rem(plane + planes // 2, planes)}
    across = {"wall": 1 - wall, "plane": plane}

    near = near_store.reshape(extent * extent * depth, near_store.shape[2])
    centre = centre_store.reshape(extent * extent * depth, near_store.shape[2])
    middle = depth // 2
    halves = [pl.multiple_of(wall * middle, middle), pl.multiple_of((1 - wall) * middle, middle)]
    near_at = 2 - 2 * wall
    fetches = [
        pltpu.make_async_copy(previous_far, previous, copy_sems.at[0]),
        pltpu.make_async_copy(length_far, length, copy_sems.at[1]),
    ]
    for at, part in enumerate(halves):
        levels_here = pl.ds(part, middle)
        fetches.append(
            pltpu.make_async_copy(
                jacobian.at[1, :, levels_here], centre_store.at[:, levels_here], copy_sems.at[2 + 2 * at]
            )
        )
        fetches.append(
            pltpu.make_async_copy(
                jacobian.at[near_at, :, levels_here],
                near_store.at[:, levels_here],
                copy_sems.at[3 + 2 * at],
            )
        )
    first_fetch = pltpu.make_async_copy(
        jacobian.at[0, :, pl.ds(0, middle)], first, copy_sems.at[6]
    )
    late = [
        pltpu.make_async_copy(residual_far, residual, copy_sems.at[7]),
        pltpu.make_async_copy(coupling_far, coupling, copy_sems.at[8]),
        pltpu.make_async_copy(partner_far, partner_map, copy_sems.at[9]),
        pltpu.make_async_copy(flag_far, flag, copy_sems.at[10]),
    ]
    fetches[1].start()
    fetches[2].start()
    fetches[3].start()
    fetches[0].start()

    barrier = pltpu.get_barrier_semaphore()

    def greet(device):
        pl.semaphore_signal(barrier, inc=1, device_id=device, device_id_type=MESH)

    greet(across)
    pl.when(wall == 0)(lambda: greet(mirror))
    pl.when(has_left)(lambda: greet(left))
    pl.when(has_right)(lambda: greet(right))
    greetings = (
        1 + (wall == 0).astype(jnp.int32) + has_left.astype(jnp.int32) + has_right.astype(jnp.int32)
    )

    @pl.when(jnp.logical_not(has_left))
    def _():
        from_left[...] = jnp.zeros_like(from_left)

    @pl.when(jnp.logical_not(has_right))
    def _():
        from_right[...] = jnp.zeros_like(from_right)

    def send(origin, target, number, device):
        return pltpu.make_async_remote_copy(
            src_ref=origin,
            dst_ref=target,
            send_sem=send_sems.at[number],
            recv_sem=recv_sems.at[number],
            device_id=device,
            device_id_type=MESH,
        )

    to_right = send(previous, from_left, 0, right)
    to_left = send(previous, from_right, 1, left)
    to_mirror = send(bottom, facing, 2, mirror)
    fetches[1].wait()

    lengths = length[...]
    base = wall * depth

    def level_at(step):
        return step + wall * (depth - 1 - 2 * step)

    def mask_at(level):
        return jnp.where(level < lengths, 1.0, 0.0).astype(jnp.float32)

    place = lax.broadcasted_iota(jnp.int32, (extent, lengths.shape[1]), 0)

    def diagonal(step, row):
        level = level_at(step)
        mask = mask_at(level + base)
        block = centre[pl.ds(row * extent * depth + level, extent, stride=depth), :]
        return block * mask + jnp.where(place == row, 1.0 - mask, 0.0)

    fetches[2].wait()
    started = [diagonal(0, row) for row in range(extent)]
    state = (
        tuple(block[:half] for block in started[:half]),
        tuple(block[half:] for block in started),
    )
    fetches[3].wait()
    fetches[4].start()
    fetches[5].start()
    pl.when(wall == 0)(first_fetch.start)
    for fetch in late:
        fetch.start()
    fetches[0].wait()
    bottom[...] = previous[pl.ds(0, extent, stride=depth), :]

    def keep_state(store, state):
        for row in range(half):
            store[row * half : (row + 1) * half, :] = state[0][row]
        for row in range(extent):
            here = (half + row) * half
            store[here : here + half, :] = state[1][row]

    def advance(step, state):
        @pl.when(step == 3)
        def _():
            pl.semaphore_wait(barrier, greetings)
            pl.when(has_right)(to_right.start)
            pl.when(has_left)(to_left.start)
            pl.when(wall == 0)(to_mirror.start)

        @pl.when(step == middle - 1)
        def _():
            fetches[4].wait()
            fetches[5].wait()

        level = level_at(step)
        start = pl.multiple_of(step * (extent * extent), extent * extent)
        mask = mask_at(level + base + 1 - wall)
        low, high = list(state[0]) + [None] * half, list(state[1])
        beyond, next_low, next_high = [], [], []
        keep_state(schur, state)
        following = jnp.minimum(step + 1, depth - 1)
        kept = jnp.where(step < depth - 1, 1.0, 0.0).astype(jnp.float32)
        for row in range(extent):
            block = near[pl.ds(row * extent * depth + level, extent, stride=depth), :] * mask
            beyond.append((block[:half], block[half:]))
            block = diagonal(following, row) * kept
            if row < half:
                next_low.append(block[:half])
            next_high.append(block[half:])
        scales = factor(low, high, beyond, (next_low, next_high))
        scale_at = pl.multiple_of(step * extent, extent)
        scale[pl.ds(scale_at, half), :] = scales[0]
        scale[pl.ds(scale_at + half, half), :] = scales[1]
        for row in range(extent):
            inverse[pl.ds(start + row * extent, half), :] = low[row]
            if row >= half:
                inverse[pl.ds(start + row * extent + half, half), :] = high[row]
            carry[pl.ds(start + row * extent, half), :] = beyond[row][0]
            carry[pl.ds(start + row * extent + half, half), :] = beyond[row][1]
        return tuple(next_low), tuple(next_high)

    change_low, change_high = lax.fori_loop(0, depth, advance, state, unroll=2)
    small = lax.broadcasted_iota(jnp.int32, change_low[0].shape, 0)
    ends = change_high[half]
    for row in range(half):
        lower_right = change_high[half + row]
        block_out[row * half : (row + 1) * half, :] = jnp.where(
            small >= row, change_low[row], lower_right
        )
        block_out[(half + row) * half : (half + row + 1) * half, :] = change_high[row]
        ends = jnp.where(small == row, lower_right, ends)
    block_out[extent * half : (extent + 1) * half, :] = ends
    to_across = send(block_out, block_in, 3, across)
    to_across.start()

    for fetch in late:
        fetch.wait()

    @pl.when(has_right)
    def _():
        to_right.wait_send()
        to_left.wait_recv()

    @pl.when(has_left)
    def _():
        to_left.wait_send()
        to_right.wait_recv()

    own = previous[...]
    span = lengths.shape[1]
    offline = (
        coupling[0] * from_left[...]
        + coupling[1] * from_right[...]
        + coupling[2] * pltpu.roll(own, 1, 1)
        + coupling[3] * pltpu.roll(own, span - 1, 1)
    )
    rows = extent * depth
    levels = lax.rem(lax.broadcasted_iota(jnp.int32, (rows, span), 0), depth) + base
    active = jnp.where(levels < lengths, 1.0, 0.0).astype(jnp.float32)
    source[...] = (residual[...] + offline) * active
    @pl.when(wall == 0)
    def _():
        first_fetch.wait()
        to_mirror.wait()
        chosen = jnp.where(
            lax.broadcasted_iota(jnp.int32, (span, span), 0) == partner_map[...], 1.0, 0.0
        ).astype(jnp.float32)
        partner = jnp.dot(
            facing[...], chosen, precision=lax.Precision.HIGHEST, preferred_element_type=jnp.float32
        )
        first_rows = first.reshape(extent * extent * middle, span)
        wake = total(
            [
                first_rows[pl.ds(inner * middle, extent, stride=extent * middle), :]
                * spread(partner, inner, extent)
                for inner in range(extent)
            ]
        )
        weight = flag[...].astype(jnp.float32)
        bottom_rows = pl.ds(0, extent, stride=depth)
        source[bottom_rows, :] = source[bottom_rows, :] - wake * weight * mask_at(base)

    def source_at(step):
        return source[pl.ds(level_at(step), extent, stride=depth), :]

    def halves_of(vector):
        return vector[:half], vector[half:]

    def spreads_of(vector):
        return [spread(vector[row // half], row % half, half) for row in range(extent)]

    def by_rows(spreads, store, start):
        return [
            total(
                [
                    spreads[row] * store[pl.ds(start + row * extent + part * half, half), :]
                    for row in range(extent)
                ]
            )
            for part in range(2)
        ]

    def by_columns(spreads, store, start):
        return [
            total(
                [
                    spreads[column]
                    * store[
                        pl.ds(start + part * half * extent + column, half, stride=extent), :
                    ]
                    for column in range(extent)
                ]
            )
            for part in range(2)
        ]

    def lower_rows(rows_low, rows_high, spreads):
        return [
            total([spreads[row] * rows_low(row) for row in range(extent)]),
            total([spreads[row] * rows_high(row) for row in range(half, extent)]),
        ]

    def forward(step, vector):
        start = pl.multiple_of(step * (extent * extent), extent * extent)
        at = pl.multiple_of(step * extent, extent)
        reduced[pl.ds(at, half), :] = vector[0]
        reduced[pl.ds(at + half, half), :] = vector[1]
        spreads = spreads_of(vector)
        lifted = [
            total(
                [
                    spreads[column]
                    * inverse[pl.ds(start + part * half * extent + column, half, stride=extent), :]
                    for column in range(half * (part + 1))
                ]
            )
            for part in range(2)
        ]
        for part in range(2):
            here = pl.ds(at + part * half, half)
            fixed[here, :] = lifted[part] * scale[here, :]
        change = by_rows(spreads_of(lifted), carry, start)
        vector_out[0:half, :] = change[0]
        vector_out[half:extent, :] = change[1]
        following = halves_of(source_at(jnp.minimum(step + 1, depth - 1)))
        return tuple(given - less for given, less in zip(following, change))

    lax.fori_loop(0, depth, forward, halves_of(source_at(0)), unroll=4)
    vector_across = send(vector_out, vector_in, 4, across)
    vector_across.start()

    to_across.wait()
    last = (depth - 1) * extent * extent
    ends = block_in[extent * half : (extent + 1) * half, :]
    low, high = [], []
    for row in range(extent):
        at = row * half
        low.append(schur[at : at + half, :] + block_in[at : at + half, :] if row < half else None)
        if row < half:
            here = (half + row) * half
            high.append(schur[here : here + half, :] + block_in[here : here + half, :])
        else:
            here = (half + row) * half
            column = block_in[pl.ds(row - half, half, stride=half), :]
            high.append(schur[here : here + half, :] + jnp.where(small == row - half, ends, column))
    scales = factor(low, high, None, None)
    for row in range(extent):
        inverse[last + row * extent : last + row * extent + half, :] = low[row]
        if row >= half:
            inverse[last + row * extent + half : last + (row + 1) * extent, :] = high[row]
    vector_across.wait()
    spreads = spreads_of(
        halves_of(reduced[(depth - 1) * extent : depth * extent, :] - vector_in[...])
    )
    lifted = [
        total(
            [
                spreads[column]
                * inverse[pl.ds(last + part * half * extent + column, half, stride=extent), :]
                for column in range(half * (part + 1))
            ]
        )
        * scales[part]
        for part in range(2)
    ]

    def lowered(vector, start):
        return lower_rows(
            lambda row: inverse[pl.ds(start + row * extent, half), :],
            lambda row: inverse[pl.ds(start + row * extent + half, half), :],
            spreads_of(vector),
        )

    def put(step, value):
        out[pl.ds(level_at(step), half, stride=depth), :] = value[0]
        out[pl.ds(level_at(step) + half * depth, half, stride=depth), :] = value[1]

    value = lowered(lifted, last)
    put(depth - 1, value)

    def backward(count, value):
        step = depth - 2 - count
        start = pl.multiple_of(step * (extent * extent), extent * extent)
        at = pl.multiple_of(step * extent, extent)
        change = by_columns(spreads_of(value), carry, start)
        given = [fixed[pl.ds(at + part * half, half), :] - change[part] for part in range(2)]
        value = lowered(given, start)
        put(step, value)
        return tuple(value)

    lax.fori_loop(0, depth - 1, backward, tuple(value), unroll=5)


def per_device(
    jacobian, residual, previous_update, offline_coupling, wake_partner, line_length, bottom_flag
):
    extent, depth, span = jacobian.shape[1], jacobian.shape[3], jacobian.shape[5]
    block = extent * extent
    whole = pl.BlockSpec(memory_space=pltpu.VMEM)
    f32 = jnp.float32

    def room(rows):
        return pltpu.VMEM((rows, span), f32)

    result = pl.pallas_call(
        functools.partial(kernel, extent, depth),
        out_shape=pltpu.VMEM((extent * depth, span), f32),
        in_specs=[pl.BlockSpec(memory_space=pl.ANY)] * 7,
        out_specs=whole,
        scratch_shapes=[
            room(extent * depth),
            room(extent * depth),
            pltpu.VMEM((4, extent * depth, span), f32),
            pltpu.VMEM((1, span), jnp.int32),
            pltpu.VMEM((1, span), jnp.int32),
            pltpu.VMEM((1, span), jnp.int32),
            pltpu.VMEM((block, depth, span), f32),
            pltpu.VMEM((block, depth, span), f32),
            pltpu.VMEM((block, depth // 2, span), f32),
            room(block * 3 // 4),
            room(block * depth),
            room(block * depth),
            room(extent * depth),
            room(extent * depth),
            room(extent * depth),
            room(extent * depth),
            room(extent),
            room(extent),
            room(extent * depth),
            room(extent * depth),
            room((extent + 1) * extent // 2),
            room((extent + 1) * extent // 2),
            room(extent),
            room(extent),
            pltpu.SemaphoreType.DMA((11,)),
            pltpu.SemaphoreType.DMA((5,)),
            pltpu.SemaphoreType.DMA((5,)),
        ],
        compiler_params=pltpu.CompilerParams(
            collective_id=0, has_side_effects=True, vmem_limit_bytes=63 * 1024 * 1024
        ),
    )(
        jacobian.reshape(3, block, depth, span),
        residual.reshape(extent * depth, span),
        previous_update.reshape(extent * depth, span),
        offline_coupling.reshape(4, extent * depth, span),
        wake_partner,
        line_length,
        bottom_flag,
    )
    return result.reshape(extent, depth, 1, span)


def solution(mesh):
    return jax.shard_map(
        per_device,
        mesh=mesh,
        in_specs=(
            P(None, None, None, "wall", "plane", None),
            P(None, "wall", "plane", None),
            P(None, "wall", "plane", None),
            P(None, None, "wall", "plane", None),
            P("plane", None),
            P("plane", None),
            P("plane", None),
        ),
        out_specs=P(None, "wall", "plane", None),
        check_vma=False,
    )
```

```python
import functools

import jax
import jax.numpy as jnp
from jax import lax
from jax.experimental import pallas as pl
from jax.experimental.pallas import tpu as pltpu
from jax.sharding import PartitionSpec as P

MESH = pl.DeviceIdType.MESH


def spread(row, index, rows):
    return jnp.broadcast_to(row[index : index + 1, :], (rows, row.shape[1]))


def factor(low, high, right, following, plain_rows):
    extent = len(high)
    half = high[0].shape[0]
    group = 4
    place = lax.broadcasted_iota(jnp.int32, high[0].shape, 0)
    scales = [jnp.zeros_like(high[0]), jnp.zeros_like(high[0])]

    def entry(row, column):
        return spread(low[row] if column < half else high[row], column % half, half)

    inverse = 1.0 / entry(0, 0)
    finished = []
    for pivot in range(extent):
        in_low = pivot < half
        at = pivot % half
        here = place == at
        pivot_low, pivot_high = low[pivot], high[pivot]
        if pivot + 1 < extent:
            beside = entry(pivot, pivot + 1)
            next_inverse = 1.0 / (entry(pivot + 1, pivot + 1) - beside * (beside * inverse))
        scales[pivot // half] = jnp.where(here, inverse, scales[pivot // half])
        scaled_low, scaled_high = pivot_low * inverse, pivot_high * inverse
        if in_low:
            scaled_low = jnp.where(here, inverse, scaled_low)
            known_low = jnp.where(place <= at, scaled_low, 0.0)
            low[pivot] = jnp.where(place < at, pivot_low, jnp.where(here, 1.0, 0.0))
            high[pivot] = None
        else:
            scaled_high = jnp.where(here, inverse, scaled_high)
            high[pivot] = jnp.where(place < at, pivot_high, jnp.where(here, 1.0, 0.0))
        if right is not None:
            scaled_right = tuple(part * inverse for part in right[pivot])
            finished.append((pivot * extent, scaled_right))
            for part in range(2):
                at_part = pivot * extent + part * half
                plain_rows[at_part : at_part + half, :] = right[pivot][part]
            right[pivot] = scaled_right
        for row in range(pivot + 1, extent):
            by = spread(pivot_low if row < half else pivot_high, row % half, half)
            if row < half:
                low[row] = jnp.where(here, 0.0, low[row]) - by * scaled_low
                high[row] = high[row] - by * scaled_high
            elif in_low:
                low[row] = -(by * known_low) if pivot == 0 else low[row] - by * known_low
                high[row] = high[row] - by * scaled_high
            else:
                low[row] = low[row] - by * scaled_low
                high[row] = jnp.where(here, 0.0, high[row]) - by * scaled_high
            if right is not None:
                right[row] = tuple(
                    part - by * scaled for part, scaled in zip(right[row], scaled_right)
                )
        if len(finished) == group:
            next_low, next_high = following
            for row in range(extent):
                bys = [
                    jnp.broadcast_to(plain_rows[start + row : start + row + 1, :], place.shape)
                    for start, _ in finished
                ]
                if row < half:
                    next_low[row] = next_low[row] - total(
                        [by * scaled[0] for by, (_, scaled) in zip(bys, finished)]
                    )
                next_high[row] = next_high[row] - total(
                    [by * scaled[1] for by, (_, scaled) in zip(bys, finished)]
                )
            finished = []
        inverse = next_inverse
    return scales


def total(terms):
    while len(terms) > 1:
        terms = [
            terms[at] + terms[at + 1] if at + 1 < len(terms) else terms[at]
            for at in range(0, len(terms), 2)
        ]
    return terms[0]


def kernel(
    extent,
    depth,
    jacobian,
    residual_far,
    previous_far,
    coupling_far,
    partner_far,
    length_far,
    flag_far,
    out,
    residual,
    previous,
    coupling,
    partner_map,
    length,
    flag,
    near_store,
    centre_store,
    first,
    schur,
    inverse,
    carry,
    source,
    reduced,
    fixed,
    scale,
    plain_rows,
    bottom,
    facing,
    from_left,
    from_right,
    block_out,
    block_in,
    vector_out,
    vector_in,
    copy_sems,
    send_sems,
    recv_sems,
):
    wall = lax.axis_index("wall")
    plane = lax.axis_index("plane")
    planes = lax.axis_size("plane")
    half = extent // 2
    has_left, has_right = plane > 0, plane < planes - 1
    right = {"wall": wall, "plane": plane + 1}
    left = {"wall": wall, "plane": plane - 1}
    mirror = {"wall": wall, "plane": lax.rem(plane + planes // 2, planes)}
    across = {"wall": 1 - wall, "plane": plane}

    near = near_store.reshape(extent * extent * depth, near_store.shape[2])
    centre = centre_store.reshape(extent * extent * depth, near_store.shape[2])
    middle = depth // 2
    halves = [pl.multiple_of(wall * middle, middle), pl.multiple_of((1 - wall) * middle, middle)]
    near_at = 2 - 2 * wall
    fetches = [
        pltpu.make_async_copy(previous_far, previous, copy_sems.at[0]),
        pltpu.make_async_copy(length_far, length, copy_sems.at[1]),
    ]
    for at, part in enumerate(halves):
        levels_here = pl.ds(part, middle)
        fetches.append(
            pltpu.make_async_copy(
                jacobian.at[1, :, levels_here], centre_store.at[:, levels_here], copy_sems.at[2 + 2 * at]
            )
        )
        fetches.append(
            pltpu.make_async_copy(
                jacobian.at[near_at, :, levels_here],
                near_store.at[:, levels_here],
                copy_sems.at[3 + 2 * at],
            )
        )
    first_fetch = pltpu.make_async_copy(
        jacobian.at[0, :, pl.ds(0, middle)], first, copy_sems.at[6]
    )
    late = [
        pltpu.make_async_copy(residual_far, residual, copy_sems.at[7]),
        pltpu.make_async_copy(coupling_far, coupling, copy_sems.at[8]),
        pltpu.make_async_copy(partner_far, partner_map, copy_sems.at[9]),
        pltpu.make_async_copy(flag_far, flag, copy_sems.at[10]),
    ]
    fetches[1].start()
    fetches[2].start()
    fetches[3].start()
    fetches[0].start()

    barrier = pltpu.get_barrier_semaphore()

    def greet(device):
        pl.semaphore_signal(barrier, inc=1, device_id=device, device_id_type=MESH)

    greet(across)
    pl.when(wall == 0)(lambda: greet(mirror))
    pl.when(has_left)(lambda: greet(left))
    pl.when(has_right)(lambda: greet(right))
    greetings = (
        1 + (wall == 0).astype(jnp.int32) + has_left.astype(jnp.int32) + has_right.astype(jnp.int32)
    )

    @pl.when(jnp.logical_not(has_left))
    def _():
        from_left[...] = jnp.zeros_like(from_left)

    @pl.when(jnp.logical_not(has_right))
    def _():
        from_right[...] = jnp.zeros_like(from_right)

    def send(origin, target, number, device):
        return pltpu.make_async_remote_copy(
            src_ref=origin,
            dst_ref=target,
            send_sem=send_sems.at[number],
            recv_sem=recv_sems.at[number],
            device_id=device,
            device_id_type=MESH,
        )

    to_right = send(previous, from_left, 0, right)
    to_left = send(previous, from_right, 1, left)
    to_mirror = send(bottom, facing, 2, mirror)
    fetches[1].wait()

    lengths = length[...]
    base = wall * depth

    def level_at(step):
        return step + wall * (depth - 1 - 2 * step)

    def mask_at(level):
        return jnp.where(level < lengths, 1.0, 0.0).astype(jnp.float32)

    place = lax.broadcasted_iota(jnp.int32, (extent, lengths.shape[1]), 0)

    def diagonal(step, row):
        level = level_at(step)
        mask = mask_at(level + base)
        block = centre[pl.ds(row * extent * depth + level, extent, stride=depth), :]
        return block * mask + jnp.where(place == row, 1.0 - mask, 0.0)

    fetches[2].wait()
    started = [diagonal(0, row) for row in range(extent)]
    state = (
        tuple(block[:half] for block in started[:half]),
        tuple(block[half:] for block in started),
    )
    fetches[3].wait()
    fetches[4].start()
    fetches[5].start()
    pl.when(wall == 0)(first_fetch.start)
    for fetch in late:
        fetch.start()
    fetches[0].wait()
    bottom[...] = previous[pl.ds(0, extent, stride=depth), :]

    def keep_state(store, state):
        for row in range(half):
            store[row * half : (row + 1) * half, :] = state[0][row]
        for row in range(extent):
            here = (half + row) * half
            store[here : here + half, :] = state[1][row]

    def advance(step, state):
        @pl.when(step == 3)
        def _():
            pl.semaphore_wait(barrier, greetings)
            pl.when(has_right)(to_right.start)
            pl.when(has_left)(to_left.start)
            pl.when(wall == 0)(to_mirror.start)

        @pl.when(step == middle - 1)
        def _():
            fetches[4].wait()
            fetches[5].wait()

        level = level_at(step)
        start = pl.multiple_of(step * (extent * extent), extent * extent)
        mask = mask_at(level + base + 1 - wall)
        low, high = list(state[0]) + [None] * half, list(state[1])
        beyond, next_low, next_high = [], [], []
        keep_state(schur, state)
        following = jnp.minimum(step + 1, depth - 1)
        kept = jnp.where(step < depth - 1, 1.0, 0.0).astype(jnp.float32)
        for row in range(extent):
            block = near[pl.ds(row * extent * depth + level, extent, stride=depth), :] * mask
            beyond.append((block[:half], block[half:]))
            block = diagonal(following, row) * kept
            if row < half:
                next_low.append(block[:half])
            next_high.append(block[half:])
        scales = factor(low, high, beyond, (next_low, next_high), plain_rows)
        scale_at = pl.multiple_of(step * extent, extent)
        scale[pl.ds(scale_at, half), :] = scales[0]
        scale[pl.ds(scale_at + half, half), :] = scales[1]
        for row in range(extent):
            inverse[pl.ds(start + row * extent, half), :] = low[row]
            if row >= half:
                inverse[pl.ds(start + row * extent + half, half), :] = high[row]
            carry[pl.ds(start + row * extent, half), :] = beyond[row][0]
            carry[pl.ds(start + row * extent + half, half), :] = beyond[row][1]
        return tuple(next_low), tuple(next_high)

    change_low, change_high = lax.fori_loop(0, depth, advance, state, unroll=2)
    small = lax.broadcasted_iota(jnp.int32, change_low[0].shape, 0)
    ends = change_high[half]
    for row in range(half):
        lower_right = change_high[half + row]
        block_out[row * half : (row + 1) * half, :] = jnp.where(
            small >= row, change_low[row], lower_right
        )
        block_out[(half + row) * half : (half + row + 1) * half, :] = change_high[row]
        ends = jnp.where(small == row, lower_right, ends)
    block_out[extent * half : (extent + 1) * half, :] = ends
    to_across = send(block_out, block_in, 3, across)
    to_across.start()

    for fetch in late:
        fetch.wait()

    @pl.when(has_right)
    def _():
        to_right.wait_send()
        to_left.wait_recv()

    @pl.when(has_left)
    def _():
        to_left.wait_send()
        to_right.wait_recv()

    own = previous[...]
    span = lengths.shape[1]
    offline = (
        coupling[0] * from_left[...]
        + coupling[1] * from_right[...]
        + coupling[2] * pltpu.roll(own, 1, 1)
        + coupling[3] * pltpu.roll(own, span - 1, 1)
    )
    rows = extent * depth
    levels = lax.rem(lax.broadcasted_iota(jnp.int32, (rows, span), 0), depth) + base
    active = jnp.where(levels < lengths, 1.0, 0.0).astype(jnp.float32)
    source[...] = (residual[...] + offline) * active
    @pl.when(wall == 0)
    def _():
        first_fetch.wait()
        to_mirror.wait()
        chosen = jnp.where(
            lax.broadcasted_iota(jnp.int32, (span, span), 0) == partner_map[...], 1.0, 0.0
        ).astype(jnp.float32)
        partner = jnp.dot(
            facing[...], chosen, precision=lax.Precision.HIGHEST, preferred_element_type=jnp.float32
        )
        first_rows = first.reshape(extent * extent * middle, span)
        wake = total(
            [
                first_rows[pl.ds(inner * middle, extent, stride=extent * middle), :]
                * spread(partner, inner, extent)
                for inner in range(extent)
            ]
        )
        weight = flag[...].astype(jnp.float32)
        bottom_rows = pl.ds(0, extent, stride=depth)
        source[bottom_rows, :] = source[bottom_rows, :] - wake * weight * mask_at(base)

    def source_at(step):
        return source[pl.ds(level_at(step), extent, stride=depth), :]

    def halves_of(vector):
        return vector[:half], vector[half:]

    def spreads_of(vector):
        return [spread(vector[row // half], row % half, half) for row in range(extent)]

    def by_rows(spreads, store, start):
        return [
            total(
                [
                    spreads[row] * store[pl.ds(start + row * extent + part * half, half), :]
                    for row in range(extent)
                ]
            )
            for part in range(2)
        ]

    def by_columns(spreads, store, start):
        return [
            total(
                [
                    spreads[column]
                    * store[
                        pl.ds(start + part * half * extent + column, half, stride=extent), :
                    ]
                    for column in range(extent)
                ]
            )
            for part in range(2)
        ]

    def lower_rows(rows_low, rows_high, spreads):
        return [
            total([spreads[row] * rows_low(row) for row in range(extent)]),
            total([spreads[row] * rows_high(row) for row in range(half, extent)]),
        ]

    def forward(step, vector):
        start = pl.multiple_of(step * (extent * extent), extent * extent)
        at = pl.multiple_of(step * extent, extent)
        reduced[pl.ds(at, half), :] = vector[0]
        reduced[pl.ds(at + half, half), :] = vector[1]
        spreads = spreads_of(vector)
        lifted = [
            total(
                [
                    spreads[column]
                    * inverse[pl.ds(start + part * half * extent + column, half, stride=extent), :]
                    for column in range(half * (part + 1))
                ]
            )
            for part in range(2)
        ]
        for part in range(2):
            here = pl.ds(at + part * half, half)
            fixed[here, :] = lifted[part] * scale[here, :]
        change = by_rows(spreads_of(lifted), carry, start)
        vector_out[0:half, :] = change[0]
        vector_out[half:extent, :] = change[1]
        following = halves_of(source_at(jnp.minimum(step + 1, depth - 1)))
        return tuple(given - less for given, less in zip(following, change))

    lax.fori_loop(0, depth, forward, halves_of(source_at(0)), unroll=4)
    vector_across = send(vector_out, vector_in, 4, across)
    vector_across.start()

    to_across.wait()
    last = (depth - 1) * extent * extent
    ends = block_in[extent * half : (extent + 1) * half, :]
    low, high = [], []
    for row in range(extent):
        at = row * half
        low.append(schur[at : at + half, :] + block_in[at : at + half, :] if row < half else None)
        if row < half:
            here = (half + row) * half
            high.append(schur[here : here + half, :] + block_in[here : here + half, :])
        else:
            here = (half + row) * half
            column = block_in[pl.ds(row - half, half, stride=half), :]
            high.append(schur[here : here + half, :] + jnp.where(small == row - half, ends, column))
    scales = factor(low, high, None, None, None)
    for row in range(extent):
        inverse[last + row * extent : last + row * extent + half, :] = low[row]
        if row >= half:
            inverse[last + row * extent + half : last + (row + 1) * extent, :] = high[row]
    vector_across.wait()
    spreads = spreads_of(
        halves_of(reduced[(depth - 1) * extent : depth * extent, :] - vector_in[...])
    )
    lifted = [
        total(
            [
                spreads[column]
                * inverse[pl.ds(last + part * half * extent + column, half, stride=extent), :]
                for column in range(half * (part + 1))
            ]
        )
        * scales[part]
        for part in range(2)
    ]

    def lowered(vector, start):
        return lower_rows(
            lambda row: inverse[pl.ds(start + row * extent, half), :],
            lambda row: inverse[pl.ds(start + row * extent + half, half), :],
            spreads_of(vector),
        )

    def put(step, value):
        out[pl.ds(level_at(step), half, stride=depth), :] = value[0]
        out[pl.ds(level_at(step) + half * depth, half, stride=depth), :] = value[1]

    value = lowered(lifted, last)
    put(depth - 1, value)

    def backward(count, value):
        step = depth - 2 - count
        start = pl.multiple_of(step * (extent * extent), extent * extent)
        at = pl.multiple_of(step * extent, extent)
        change = by_columns(spreads_of(value), carry, start)
        given = [fixed[pl.ds(at + part * half, half), :] - change[part] for part in range(2)]
        value = lowered(given, start)
        put(step, value)
        return tuple(value)

    lax.fori_loop(0, depth - 1, backward, tuple(value), unroll=5)


def per_device(
    jacobian, residual, previous_update, offline_coupling, wake_partner, line_length, bottom_flag
):
    extent, depth, span = jacobian.shape[1], jacobian.shape[3], jacobian.shape[5]
    block = extent * extent
    whole = pl.BlockSpec(memory_space=pltpu.VMEM)
    f32 = jnp.float32

    def room(rows):
        return pltpu.VMEM((rows, span), f32)

    result = pl.pallas_call(
        functools.partial(kernel, extent, depth),
        out_shape=pltpu.VMEM((extent * depth, span), f32),
        in_specs=[pl.BlockSpec(memory_space=pl.ANY)] * 7,
        out_specs=whole,
        scratch_shapes=[
            room(extent * depth),
            room(extent * depth),
            pltpu.VMEM((4, extent * depth, span), f32),
            pltpu.VMEM((1, span), jnp.int32),
            pltpu.VMEM((1, span), jnp.int32),
            pltpu.VMEM((1, span), jnp.int32),
            pltpu.VMEM((block, depth, span), f32),
            pltpu.VMEM((block, depth, span), f32),
            pltpu.VMEM((block, depth // 2, span), f32),
            room(block * 3 // 4),
            room(block * depth),
            room(block * depth),
            room(extent * depth),
            room(extent * depth),
            room(extent * depth),
            room(extent * depth),
            room(block),
            room(extent),
            room(extent),
            room(extent * depth),
            room(extent * depth),
            room((extent + 1) * extent // 2),
            room((extent + 1) * extent // 2),
            room(extent),
            room(extent),
            pltpu.SemaphoreType.DMA((11,)),
            pltpu.SemaphoreType.DMA((5,)),
            pltpu.SemaphoreType.DMA((5,)),
        ],
        compiler_params=pltpu.CompilerParams(
            collective_id=0, has_side_effects=True, vmem_limit_bytes=63 * 1024 * 1024
        ),
    )(
        jacobian.reshape(3, block, depth, span),
        residual.reshape(extent * depth, span),
        previous_update.reshape(extent * depth, span),
        offline_coupling.reshape(4, extent * depth, span),
        wake_partner,
        line_length,
        bottom_flag,
    )
    return result.reshape(extent, depth, 1, span)


def solution(mesh):
    return jax.shard_map(
        per_device,
        mesh=mesh,
        in_specs=(
            P(None, None, None, "wall", "plane", None),
            P(None, "wall", "plane", None),
            P(None, "wall", "plane", None),
            P(None, None, "wall", "plane", None),
            P("plane", None),
            P("plane", None),
            P("plane", None),
        ),
        out_specs=P(None, "wall", "plane", None),
        check_vma=False,
    )
```

```python
import functools

import jax
import jax.numpy as jnp
from jax import lax
from jax.experimental import pallas as pl
from jax.experimental.pallas import tpu as pltpu
from jax.sharding import PartitionSpec as P

MESH = pl.DeviceIdType.MESH


def spread(row, index, rows):
    return jnp.broadcast_to(row[index : index + 1, :], (rows, row.shape[1]))


def factor(low, high, right, following, plain_rows):
    extent = len(high)
    half = high[0].shape[0]
    group = 4
    place = lax.broadcasted_iota(jnp.int32, high[0].shape, 0)
    scales = [jnp.zeros_like(high[0]), jnp.zeros_like(high[0])]

    def entry(row, column):
        return spread(low[row] if column < half else high[row], column % half, half)

    inverse = 1.0 / entry(0, 0)
    finished = []
    for pivot in range(extent):
        in_low = pivot < half
        at = pivot % half
        here = place == at
        pivot_low, pivot_high = low[pivot], high[pivot]
        if pivot + 1 < extent:
            beside = entry(pivot, pivot + 1)
            next_inverse = 1.0 / (entry(pivot + 1, pivot + 1) - beside * (beside * inverse))
        scales[pivot // half] = jnp.where(here, inverse, scales[pivot // half])
        scaled_low, scaled_high = pivot_low * inverse, pivot_high * inverse
        if in_low:
            scaled_low = jnp.where(here, inverse, scaled_low)
            known_low = jnp.where(place <= at, scaled_low, 0.0)
            low[pivot] = jnp.where(place < at, pivot_low, jnp.where(here, 1.0, 0.0))
            high[pivot] = None
        else:
            scaled_high = jnp.where(here, inverse, scaled_high)
            high[pivot] = jnp.where(place < at, pivot_high, jnp.where(here, 1.0, 0.0))
        if right is not None:
            scaled_right = tuple(part * inverse for part in right[pivot])
            finished.append((pivot * extent, scaled_right))
            for part in range(2):
                at_part = pivot * extent + part * half
                plain_rows[at_part : at_part + half, :] = right[pivot][part]
            right[pivot] = scaled_right
        for row in range(pivot + 1, extent):
            by = spread(pivot_low if row < half else pivot_high, row % half, half)
            if row < half:
                low[row] = jnp.where(here, 0.0, low[row]) - by * scaled_low
                high[row] = high[row] - by * scaled_high
            elif in_low:
                low[row] = -(by * known_low) if pivot == 0 else low[row] - by * known_low
                high[row] = high[row] - by * scaled_high
            else:
                low[row] = low[row] - by * scaled_low
                high[row] = jnp.where(here, 0.0, high[row]) - by * scaled_high
            if right is not None:
                right[row] = tuple(
                    part - by * scaled for part, scaled in zip(right[row], scaled_right)
                )
        if len(finished) == group:
            next_low, next_high = following
            for row in range(extent):
                bys = [
                    jnp.broadcast_to(plain_rows[start + row : start + row + 1, :], place.shape)
                    for start, _ in finished
                ]
                if row < half:
                    next_low[row] = next_low[row] - total(
                        [by * scaled[0] for by, (_, scaled) in zip(bys, finished)]
                    )
                next_high[row] = next_high[row] - total(
                    [by * scaled[1] for by, (_, scaled) in zip(bys, finished)]
                )
            finished = []
        inverse = next_inverse
    return scales


def total(terms):
    while len(terms) > 1:
        terms = [
            terms[at] + terms[at + 1] if at + 1 < len(terms) else terms[at]
            for at in range(0, len(terms), 2)
        ]
    return terms[0]


def kernel(
    extent,
    depth,
    jacobian,
    residual_far,
    previous_far,
    coupling_far,
    partner_far,
    length_far,
    flag_far,
    out,
    residual,
    previous,
    coupling,
    partner_map,
    length,
    flag,
    near_store,
    centre_store,
    first,
    schur,
    inverse,
    carry,
    source,
    reduced,
    fixed,
    scale,
    plain_rows,
    bottom,
    facing,
    from_left,
    from_right,
    block_out,
    block_in,
    vector_out,
    vector_in,
    copy_sems,
    send_sems,
    recv_sems,
):
    wall = lax.axis_index("wall")
    plane = lax.axis_index("plane")
    planes = lax.axis_size("plane")
    half = extent // 2
    has_left, has_right = plane > 0, plane < planes - 1
    right = {"wall": wall, "plane": plane + 1}
    left = {"wall": wall, "plane": plane - 1}
    mirror = {"wall": wall, "plane": lax.rem(plane + planes // 2, planes)}
    across = {"wall": 1 - wall, "plane": plane}

    near = near_store.reshape(extent * extent * depth, near_store.shape[2])
    centre = centre_store.reshape(extent * extent * depth, near_store.shape[2])
    middle = depth // 2
    halves = [pl.multiple_of(wall * middle, middle), pl.multiple_of((1 - wall) * middle, middle)]
    near_at = 2 - 2 * wall
    fetches = [
        pltpu.make_async_copy(previous_far, previous, copy_sems.at[0]),
        pltpu.make_async_copy(length_far, length, copy_sems.at[1]),
    ]
    for at, part in enumerate(halves):
        levels_here = pl.ds(part, middle)
        fetches.append(
            pltpu.make_async_copy(
                jacobian.at[1, :, levels_here], centre_store.at[:, levels_here], copy_sems.at[2 + 2 * at]
            )
        )
        fetches.append(
            pltpu.make_async_copy(
                jacobian.at[near_at, :, levels_here],
                near_store.at[:, levels_here],
                copy_sems.at[3 + 2 * at],
            )
        )
    first_fetch = pltpu.make_async_copy(
        jacobian.at[0, :, pl.ds(0, middle)], first, copy_sems.at[6]
    )
    late = [
        pltpu.make_async_copy(residual_far, residual, copy_sems.at[7]),
        pltpu.make_async_copy(coupling_far, coupling, copy_sems.at[8]),
        pltpu.make_async_copy(partner_far, partner_map, copy_sems.at[9]),
        pltpu.make_async_copy(flag_far, flag, copy_sems.at[10]),
    ]
    fetches[1].start()
    fetches[2].start()
    fetches[3].start()
    fetches[0].start()

    barrier = pltpu.get_barrier_semaphore()

    def greet(device):
        pl.semaphore_signal(barrier, inc=1, device_id=device, device_id_type=MESH)

    greet(across)
    pl.when(wall == 0)(lambda: greet(mirror))
    pl.when(has_left)(lambda: greet(left))
    pl.when(has_right)(lambda: greet(right))
    greetings = (
        1 + (wall == 0).astype(jnp.int32) + has_left.astype(jnp.int32) + has_right.astype(jnp.int32)
    )

    @pl.when(jnp.logical_not(has_left))
    def _():
        from_left[...] = jnp.zeros_like(from_left)

    @pl.when(jnp.logical_not(has_right))
    def _():
        from_right[...] = jnp.zeros_like(from_right)

    def send(origin, target, number, device):
        return pltpu.make_async_remote_copy(
            src_ref=origin,
            dst_ref=target,
            send_sem=send_sems.at[number],
            recv_sem=recv_sems.at[number],
            device_id=device,
            device_id_type=MESH,
        )

    to_right = send(previous, from_left, 0, right)
    to_left = send(previous, from_right, 1, left)
    to_mirror = send(bottom, facing, 2, mirror)
    fetches[1].wait()

    lengths = length[...]
    base = wall * depth

    def level_at(step):
        return step + wall * (depth - 1 - 2 * step)

    def mask_at(level):
        return jnp.where(level < lengths, 1.0, 0.0).astype(jnp.float32)

    place = lax.broadcasted_iota(jnp.int32, (extent, lengths.shape[1]), 0)

    def diagonal(step, row):
        level = level_at(step)
        mask = mask_at(level + base)
        block = centre[pl.ds(row * extent * depth + level, extent, stride=depth), :]
        return block * mask + jnp.where(place == row, 1.0 - mask, 0.0)

    fetches[2].wait()
    started = [diagonal(0, row) for row in range(extent)]
    state = (
        tuple(block[:half] for block in started[:half]),
        tuple(block[half:] for block in started),
    )
    fetches[3].wait()
    fetches[4].start()
    fetches[5].start()
    pl.when(wall == 0)(first_fetch.start)
    for fetch in late:
        fetch.start()
    fetches[0].wait()
    bottom[...] = previous[pl.ds(0, extent, stride=depth), :]

    def keep_state(store, state):
        for row in range(half):
            store[row * half : (row + 1) * half, :] = state[0][row]
        for row in range(extent):
            here = (half + row) * half
            store[here : here + half, :] = state[1][row]

    def advance(step, state):
        @pl.when(step == 3)
        def _():
            pl.semaphore_wait(barrier, greetings)
            pl.when(has_right)(to_right.start)
            pl.when(has_left)(to_left.start)
            pl.when(wall == 0)(to_mirror.start)

        @pl.when(step == middle - 1)
        def _():
            fetches[4].wait()
            fetches[5].wait()

        level = level_at(step)
        start = pl.multiple_of(step * (extent * extent), extent * extent)
        mask = mask_at(level + base + 1 - wall)
        low, high = list(state[0]) + [None] * half, list(state[1])
        beyond, next_low, next_high = [], [], []
        keep_state(schur, state)
        following = jnp.minimum(step + 1, depth - 1)
        kept = jnp.where(step < depth - 1, 1.0, 0.0).astype(jnp.float32)
        for row in range(extent):
            block = near[pl.ds(row * extent * depth + level, extent, stride=depth), :] * mask
            beyond.append((block[:half], block[half:]))
            block = diagonal(following, row) * kept
            if row < half:
                next_low.append(block[:half])
            next_high.append(block[half:])
        scales = factor(low, high, beyond, (next_low, next_high), plain_rows)
        scale_at = pl.multiple_of(step * extent, extent)
        scale[pl.ds(scale_at, half), :] = scales[0]
        scale[pl.ds(scale_at + half, half), :] = scales[1]
        for row in range(extent):
            inverse[pl.ds(start + row * extent, half), :] = low[row]
            if row >= half:
                inverse[pl.ds(start + row * extent + half, half), :] = high[row]
            carry[pl.ds(start + row * extent, half), :] = beyond[row][0]
            carry[pl.ds(start + row * extent + half, half), :] = beyond[row][1]
        return tuple(next_low), tuple(next_high)

    change_low, change_high = lax.fori_loop(0, depth, advance, state, unroll=4)
    small = lax.broadcasted_iota(jnp.int32, change_low[0].shape, 0)
    ends = change_high[half]
    for row in range(half):
        lower_right = change_high[half + row]
        block_out[row * half : (row + 1) * half, :] = jnp.where(
            small >= row, change_low[row], lower_right
        )
        block_out[(half + row) * half : (half + row + 1) * half, :] = change_high[row]
        ends = jnp.where(small == row, lower_right, ends)
    block_out[extent * half : (extent + 1) * half, :] = ends
    to_across = send(block_out, block_in, 3, across)
    to_across.start()

    for fetch in late:
        fetch.wait()

    @pl.when(has_right)
    def _():
        to_right.wait_send()
        to_left.wait_recv()

    @pl.when(has_left)
    def _():
        to_left.wait_send()
        to_right.wait_recv()

    own = previous[...]
    span = lengths.shape[1]
    offline = (
        coupling[0] * from_left[...]
        + coupling[1] * from_right[...]
        + coupling[2] * pltpu.roll(own, 1, 1)
        + coupling[3] * pltpu.roll(own, span - 1, 1)
    )
    rows = extent * depth
    levels = lax.rem(lax.broadcasted_iota(jnp.int32, (rows, span), 0), depth) + base
    active = jnp.where(levels < lengths, 1.0, 0.0).astype(jnp.float32)
    source[...] = (residual[...] + offline) * active
    @pl.when(wall == 0)
    def _():
        first_fetch.wait()
        to_mirror.wait()
        chosen = jnp.where(
            lax.broadcasted_iota(jnp.int32, (span, span), 0) == partner_map[...], 1.0, 0.0
        ).astype(jnp.float32)
        partner = jnp.dot(
            facing[...], chosen, precision=lax.Precision.HIGHEST, preferred_element_type=jnp.float32
        )
        first_rows = first.reshape(extent * extent * middle, span)
        wake = total(
            [
                first_rows[pl.ds(inner * middle, extent, stride=extent * middle), :]
                * spread(partner, inner, extent)
                for inner in range(extent)
            ]
        )
        weight = flag[...].astype(jnp.float32)
        bottom_rows = pl.ds(0, extent, stride=depth)
        source[bottom_rows, :] = source[bottom_rows, :] - wake * weight * mask_at(base)

    def source_at(step):
        return source[pl.ds(level_at(step), extent, stride=depth), :]

    def halves_of(vector):
        return vector[:half], vector[half:]

    def spreads_of(vector):
        return [spread(vector[row // half], row % half, half) for row in range(extent)]

    def by_rows(spreads, store, start):
        return [
            total(
                [
                    spreads[row] * store[pl.ds(start + row * extent + part * half, half), :]
                    for row in range(extent)
                ]
            )
            for part in range(2)
        ]

    def by_columns(spreads, store, start):
        return [
            total(
                [
                    spreads[column]
                    * store[
                        pl.ds(start + part * half * extent + column, half, stride=extent), :
                    ]
                    for column in range(extent)
                ]
            )
            for part in range(2)
        ]

    def lower_rows(rows_low, rows_high, spreads):
        return [
            total([spreads[row] * rows_low(row) for row in range(extent)]),
            total([spreads[row] * rows_high(row) for row in range(half, extent)]),
        ]

    def forward(step, vector):
        start = pl.multiple_of(step * (extent * extent), extent * extent)
        at = pl.multiple_of(step * extent, extent)
        reduced[pl.ds(at, half), :] = vector[0]
        reduced[pl.ds(at + half, half), :] = vector[1]
        spreads = spreads_of(vector)
        lifted = [
            total(
                [
                    spreads[column]
                    * inverse[pl.ds(start + part * half * extent + column, half, stride=extent), :]
                    for column in range(half * (part + 1))
                ]
            )
            for part in range(2)
        ]
        for part in range(2):
            here = pl.ds(at + part * half, half)
            fixed[here, :] = lifted[part] * scale[here, :]
        change = by_rows(spreads_of(lifted), carry, start)
        vector_out[0:half, :] = change[0]
        vector_out[half:extent, :] = change[1]
        following = halves_of(source_at(jnp.minimum(step + 1, depth - 1)))
        return tuple(given - less for given, less in zip(following, change))

    lax.fori_loop(0, depth, forward, halves_of(source_at(0)), unroll=4)
    vector_across = send(vector_out, vector_in, 4, across)
    vector_across.start()

    to_across.wait()
    last = (depth - 1) * extent * extent
    ends = block_in[extent * half : (extent + 1) * half, :]
    low, high = [], []
    for row in range(extent):
        at = row * half
        low.append(schur[at : at + half, :] + block_in[at : at + half, :] if row < half else None)
        if row < half:
            here = (half + row) * half
            high.append(schur[here : here + half, :] + block_in[here : here + half, :])
        else:
            here = (half + row) * half
            column = block_in[pl.ds(row - half, half, stride=half), :]
            high.append(schur[here : here + half, :] + jnp.where(small == row - half, ends, column))
    scales = factor(low, high, None, None, None)
    for row in range(extent):
        inverse[last + row * extent : last + row * extent + half, :] = low[row]
        if row >= half:
            inverse[last + row * extent + half : last + (row + 1) * extent, :] = high[row]
    vector_across.wait()
    spreads = spreads_of(
        halves_of(reduced[(depth - 1) * extent : depth * extent, :] - vector_in[...])
    )
    lifted = [
        total(
            [
                spreads[column]
                * inverse[pl.ds(last + part * half * extent + column, half, stride=extent), :]
                for column in range(half * (part + 1))
            ]
        )
        * scales[part]
        for part in range(2)
    ]

    def lowered(vector, start):
        return lower_rows(
            lambda row: inverse[pl.ds(start + row * extent, half), :],
            lambda row: inverse[pl.ds(start + row * extent + half, half), :],
            spreads_of(vector),
        )

    def put(step, value):
        out[pl.ds(level_at(step), half, stride=depth), :] = value[0]
        out[pl.ds(level_at(step) + half * depth, half, stride=depth), :] = value[1]

    value = lowered(lifted, last)
    put(depth - 1, value)

    def backward(count, value):
        step = depth - 2 - count
        start = pl.multiple_of(step * (extent * extent), extent * extent)
        at = pl.multiple_of(step * extent, extent)
        change = by_columns(spreads_of(value), carry, start)
        given = [fixed[pl.ds(at + part * half, half), :] - change[part] for part in range(2)]
        value = lowered(given, start)
        put(step, value)
        return tuple(value)

    lax.fori_loop(0, depth - 1, backward, tuple(value), unroll=5)


def per_device(
    jacobian, residual, previous_update, offline_coupling, wake_partner, line_length, bottom_flag
):
    extent, depth, span = jacobian.shape[1], jacobian.shape[3], jacobian.shape[5]
    block = extent * extent
    whole = pl.BlockSpec(memory_space=pltpu.VMEM)
    f32 = jnp.float32

    def room(rows):
        return pltpu.VMEM((rows, span), f32)

    result = pl.pallas_call(
        functools.partial(kernel, extent, depth),
        out_shape=pltpu.VMEM((extent * depth, span), f32),
        in_specs=[pl.BlockSpec(memory_space=pl.ANY)] * 7,
        out_specs=whole,
        scratch_shapes=[
            room(extent * depth),
            room(extent * depth),
            pltpu.VMEM((4, extent * depth, span), f32),
            pltpu.VMEM((1, span), jnp.int32),
            pltpu.VMEM((1, span), jnp.int32),
            pltpu.VMEM((1, span), jnp.int32),
            pltpu.VMEM((block, depth, span), f32),
            pltpu.VMEM((block, depth, span), f32),
            pltpu.VMEM((block, depth // 2, span), f32),
            room(block * 3 // 4),
            room(block * depth),
            room(block * depth),
            room(extent * depth),
            room(extent * depth),
            room(extent * depth),
            room(extent * depth),
            room(block),
            room(extent),
            room(extent),
            room(extent * depth),
            room(extent * depth),
            room((extent + 1) * extent // 2),
            room((extent + 1) * extent // 2),
            room(extent),
            room(extent),
            pltpu.SemaphoreType.DMA((11,)),
            pltpu.SemaphoreType.DMA((5,)),
            pltpu.SemaphoreType.DMA((5,)),
        ],
        compiler_params=pltpu.CompilerParams(
            collective_id=0, has_side_effects=True, vmem_limit_bytes=63 * 1024 * 1024
        ),
    )(
        jacobian.reshape(3, block, depth, span),
        residual.reshape(extent * depth, span),
        previous_update.reshape(extent * depth, span),
        offline_coupling.reshape(4, extent * depth, span),
        wake_partner,
        line_length,
        bottom_flag,
    )
    return result.reshape(extent, depth, 1, span)


def solution(mesh):
    return jax.shard_map(
        per_device,
        mesh=mesh,
        in_specs=(
            P(None, None, None, "wall", "plane", None),
            P(None, "wall", "plane", None),
            P(None, "wall", "plane", None),
            P(None, None, "wall", "plane", None),
            P("plane", None),
            P("plane", None),
            P("plane", None),
        ),
        out_specs=P(None, "wall", "plane", None),
        check_vma=False,
    )
```
